256 devices in a mesh: grp: 4 (over z_lo, core), gx: 4 (over x), gz: 16 (over z_hi, y).
Axes of the slice: x: 4, y: 4, z: 8 (z_hi: 4, z_lo: 2; z = z_hi * 2 + z_lo), core: 2. Of those that a mesh axis runs over, the one named last changes fastest.
Arguments:
- velocity: bfloat16 [3, 256, 320, 2048], P(None, ('grp', 'gx'), None, 'gz'), may hold values from -6 to 6
- base_flow: float32 [320], replicated, may hold values from 0.2 to 1.5
- wall_second: bfloat16 [320, 320], replicated, may hold values from -0.3125 to 0.3125
- wall_first: bfloat16 [320, 320], replicated, may hold values from -0.3125 to 0.3125
- rescale: bfloat16 [320, 320], replicated, may hold values from -0.3125 to 0.3125
- pressure_diag: float32 [320], replicated, may hold values from 0.05 to 1.5
Outputs:
- advanced: bfloat16 [3, 256, 320, 2048], P(None, ('grp', 'gx'), None, 'gz')
The draws below stay inside these ranges and needn't reach their ends.
All inputs are finite; a program needn't handle non-finite values.
Results may differ from the reference program's by a relative error of at most 0.0075.
Values may be sent and summed in bfloat16 or wider, within the bound.
No kernel may reach another device: no remote copies, remote signals or barrier semaphores. Data moves between devices by JAX's collectives and lax.ppermute only.
A program may use at most 128 MiB of HBM per device.

```python
import math
import jax
import jax.numpy as jnp
from jax import lax

NY = 320
XA = 64
NX = 256
NZ = 2048


def level_of(stream_key, shape, pieces, least, largest):
    def one(position, parts):
        steps = jax.random.uniform(jax.random.fold_in(jax.random.fold_in(stream_key, 6), position), (parts,), jnp.float32, least / len(pieces), largest / len(pieces))
        return jnp.repeat(jnp.exp(steps), shape[position] // parts).reshape((-1,) + (1,) * (len(shape) - position - 1))

    factor_of = one(*pieces[0])
    for cut in pieces[1:]:
        factor_of = factor_of * one(*cut)
    return factor_of


def gaussian(key, dims, scale, bound, cuts=(), kind=jnp.bfloat16):
    values = scale * jax.random.normal(key, dims, jnp.float32)
    if cuts:
        values = values * level_of(key, dims, cuts, -0.22, 0.18)
    return jnp.clip(values, -bound, bound).astype(kind)


def setup_inputs(seed: int = 0) -> dict:
    streams_of = jax.random.split(jax.random.key(seed), 7)
    velocity = gaussian(streams_of[0], (3, NX, NY, NZ), 1.0, 6.0, ((1, 16), (3, 16)))
    base_flow = jnp.clip(jax.random.uniform(streams_of[1], (NY,), jnp.float32, 0.2, 1.5), 0.2, 1.5)
    wall_second = gaussian(streams_of[2], (NY, NY), NY ** -0.5, 0.3125)
    wall_first = gaussian(streams_of[3], (NY, NY), NY ** -0.5, 0.3125)
    rescale = gaussian(streams_of[4], (NY, NY), NY ** -0.5, 0.3125)
    pressure_diag = jnp.clip(jnp.exp(jax.random.uniform(streams_of[5], (NY,), jnp.float32, math.log(0.05), math.log(1.5))), 0.05, 1.5)
    return dict(velocity=velocity, base_flow=base_flow, wall_second=wall_second, wall_first=wall_first, rescale=rescale, pressure_diag=pressure_diag)


step_size = 0.25
viscosity = 0.4

def advance(padded, base_flow, wall_second):
    widen = padded.astype(jnp.float32)
    centre = widen[:, 2:-2]
    slope = (widen[:, :-4] - 8.0 * widen[:, 1:-3] + 8.0 * widen[:, 3:-1] - widen[:, 4:]) / 12.0
    bend = (-widen[:, :-4] + 16.0 * widen[:, 1:-3] - 30.0 * centre + 16.0 * widen[:, 3:-1] - widen[:, 4:]) / 12.0
    normal = jnp.einsum('yj,cxjz->cxyz', wall_second.astype(jnp.float32), centre)
    return centre + step_size * (viscosity * (bend + normal) - base_flow[None, None, :, None] * slope)

def hartley(field):
    spectrum = jnp.fft.fft(field.astype(jnp.float32), axis=-1)
    return (spectrum.real - spectrum.imag) / math.sqrt(field.shape[-1])

def wave_numbers(count):
    index = jnp.arange(count, dtype=jnp.int32)
    signed = jnp.where(index < count // 2, index, index - count)
    signed = jnp.where(index == count // 2, 0, signed)
    slope_wave = signed.astype(jnp.float32) * (2.0 * math.pi / count)
    folded = jnp.minimum(index, count - index).astype(jnp.float32) * (2.0 * math.pi / count)
    return (slope_wave, folded * folded)

def mirror(field):
    return jnp.roll(jnp.flip(field, -1), 1, -1)

def solve_pressure(source, pressure_diag, squared):
    count_y = source.shape[1]
    centre = -(2.0 + pressure_diag[None, :] + squared[:, None])
    rows = jnp.arange(count_y, dtype=jnp.int32)
    below = jnp.broadcast_to(jnp.where(rows == 0, 0.0, 1.0).astype(centre.dtype), centre.shape)
    above = jnp.broadcast_to(jnp.where(rows == count_y - 1, 0.0, 1.0).astype(centre.dtype), centre.shape)
    solved = lax.linalg.tridiagonal_solve(below, centre, above, jnp.transpose(source, (2, 1, 0)))
    return jnp.transpose(solved, (2, 1, 0))

def project(normal_star, span_star, wall_first, pressure_diag):
    wall_slope = jnp.einsum('yj,pjz->pyz', wall_first.astype(jnp.float32), normal_star.astype(jnp.float32)).astype(jnp.bfloat16)
    slope_hat = hartley(wall_slope)
    span_hat = hartley(span_star)
    slope_wave, squared = wave_numbers(span_star.shape[-1])
    source = (slope_hat - slope_wave * mirror(span_hat)) / step_size
    pressure = solve_pressure(source, pressure_diag, squared)
    normal_part = jnp.einsum('yj,pjz->pyz', wall_first.astype(jnp.float32), pressure, precision=lax.Precision.HIGHEST).astype(jnp.bfloat16)
    span_part = (-slope_wave * mirror(pressure)).astype(jnp.bfloat16)
    normal_new = (normal_star.astype(jnp.float32) - step_size * hartley(normal_part)).astype(jnp.bfloat16)
    span_new = (span_star.astype(jnp.float32) - step_size * hartley(span_part)).astype(jnp.bfloat16)
    return (normal_new, span_new)

def reference(velocity, base_flow, wall_second, wall_first, rescale, pressure_diag):
    auxiliary = velocity[:, :XA]
    main_layer = velocity[:, XA:]
    inflow = jnp.einsum('yj,cpjz->cpyz', rescale.astype(jnp.float32), velocity[:, XA - 2:XA].astype(jnp.float32)).astype(jnp.bfloat16)
    aux_padded = jnp.concatenate([auxiliary[:, :1], auxiliary[:, :1], auxiliary, auxiliary[:, -1:], auxiliary[:, -1:]], 1)
    main_padded = jnp.concatenate([inflow, main_layer, main_layer[:, -1:], main_layer[:, -1:]], 1)
    padded = jnp.concatenate([aux_padded, main_padded], 1)

    def plane(index):
        start = (index + 4 * (index >= XA).astype(jnp.int32)).astype(jnp.int32)
        window = lax.dynamic_slice_in_dim(padded, start, 5, 1)
        provisional = advance(window, base_flow, wall_second)
        stream_star = provisional[0].astype(jnp.bfloat16)
        normal_new, span_new = project(provisional[1].astype(jnp.bfloat16), provisional[2].astype(jnp.bfloat16), wall_first, pressure_diag)
        return jnp.stack([stream_star, normal_new, span_new], 0)
    planes = lax.map(plane, jnp.arange(NX, dtype=jnp.int32))
    return jnp.transpose(planes[:, :, 0], (1, 0, 2, 3))
```

```python
import functools
import math

import jax
import jax.numpy as jnp
import ml_dtypes
import numpy as np
from jax import lax
from jax.experimental import pallas as pl
from jax.experimental.pallas import tpu as pltpu
from jax.sharding import PartitionSpec as P

step_size = 0.25
viscosity = 0.4
LANES = 128
TILE = 256
VMEM_BYTES = 56 * 1024 * 1024


def mode_columns(count):
    quarter = count // 4
    even = 2 * np.arange(quarter)
    odd = even + 1
    sine_even = even.copy()
    sine_even[0] = count // 2
    is_sine = np.concatenate([np.zeros(quarter), np.ones(quarter), np.zeros(quarter), np.ones(quarter)]).astype(bool)
    is_sine[quarter] = False
    return np.concatenate([even, sine_even, odd, odd]).astype(np.int64), is_sine


@functools.lru_cache(maxsize=None)
def tables(count):
    half = count // 2
    mode, is_sine = mode_columns(count)
    z = np.arange(half, dtype=np.int64)
    angle = (z[:, None] * mode[None, :] % count).astype(np.float64) * (2.0 * math.pi / count)
    cosine, sine = np.cos(angle), np.sin(angle)
    own = np.where(is_sine[None, :], sine, cosine) / math.sqrt(count)
    signed = np.where((mode == 0) | (mode == half), 0, mode) * (2.0 * math.pi / count)
    other = np.where(is_sine[None, :], cosine, -sine) * signed[None, :] / math.sqrt(count)
    weight = np.where((mode == 0) | (mode == half), 1.0, 2.0)
    to_modes = [own / step_size, -other / step_size]
    from_modes = [-step_size * own * weight, -step_size * other * weight]
    steps = []
    for start in range(0, count, TILE):
        steps.append(np.concatenate([t[:, start : start + TILE] for t in to_modes], 0))
    for table in from_modes:
        for start in range(0, half, TILE):
            steps.append(
                np.concatenate([table[start : start + TILE, :half].T, table[start : start + TILE, half:].T], 0)
            )
    folded = np.minimum(mode, count - mode).astype(np.float64) * (2.0 * math.pi / count)
    return (
        np.stack(steps).astype(np.float32).astype(ml_dtypes.bfloat16),
        (folded * folded).astype(np.float32).reshape(count // LANES, LANES),
    )


def advance_kernel(with_slope, flags, vel, lower, upper, flow, second, first, rescale, *rest):
    if with_slope:
        star_ref, send_ref, pad, acc = rest
    else:
        _, star_ref, pad, acc = rest
    planes = vel.shape[1]
    rows = vel.shape[2]
    pad[pl.ds(2, planes)] = vel[0]

    @pl.when(flags[0] == 0)
    def _():
        pad[0:2] = lower[0]

    @pl.when(flags[0] == 1)
    def _():
        pad[0] = vel[0, 0]
        pad[1] = vel[0, 0]

    @pl.when(flags[0] == 2)
    def _():
        both = jnp.concatenate([lower[0, 0], lower[0, 1]], 1)
        inflow = jnp.dot(rescale[...], both, preferred_element_type=jnp.float32).astype(jnp.bfloat16)
        pad[0] = inflow[:, :LANES]
        pad[1] = inflow[:, LANES:]

    @pl.when(flags[1] == 0)
    def _():
        pad[planes + 2 : planes + 4] = upper[0]

    @pl.when(flags[1] == 1)
    def _():
        pad[planes + 2] = vel[0, planes - 1]
        pad[planes + 3] = vel[0, planes - 1]

    strip = 80
    bend_scale = step_size * viscosity / 12.0
    normal_scale = step_size * viscosity

    def pair(i, carry):
        at = i * 2
        both = jnp.concatenate([pad[at + 2], pad[at + 3]], 1)
        acc[...] = jnp.dot(second[...], both, preferred_element_type=jnp.float32)
        for row in range(0, rows, strip):
            here = pl.ds(row, strip)
            ghost = [pad[at + k, here, :].astype(jnp.float32) for k in range(6)]
            for half in range(2):
                far_low, low, centre, high, far_high = ghost[half : half + 5]
                bend = 16.0 * (low + high) - (far_low + far_high) - 30.0 * centre
                slope = 8.0 * (high - low) - (far_high - far_low)
                new = (
                    centre
                    + normal_scale * acc[here, half * LANES : (half + 1) * LANES]
                    + bend_scale * bend
                    - flow[here, :] * slope
                )
                star_ref[0, at + half, here, :] = new.astype(jnp.bfloat16)
        return carry

    lax.fori_loop(0, planes // 2, pair, 0)

    if with_slope:

        @pl.when(pl.program_id(0) == 0)
        def _():
            def slope_pair(i, carry):
                at = i * 2
                both = jnp.concatenate([star_ref[0, at], star_ref[0, at + 1]], 1)
                out = jnp.dot(first[...], both, preferred_element_type=jnp.float32).astype(jnp.bfloat16)
                send_ref[at, 0] = out[:, :LANES]
                send_ref[at + 1, 0] = out[:, LANES:]
                return carry

            lax.fori_loop(0, planes // 2, slope_pair, 0)

        @pl.when(pl.program_id(0) == 1)
        def _():
            send_ref[:, 0] = star_ref[0]


def advance(flags, velocity, lower, upper, flow, second, first, rescale, star=None):
    planes, rows, lanes = velocity.shape[1:]
    with_slope = star is None
    shift = 1 if with_slope else 0
    steps = 2 if with_slope else 1
    field = lambda count, offset: pl.BlockSpec((1, count, rows, lanes), lambda c: (c + offset, 0, 0, 0))
    fixed = lambda shape: pl.BlockSpec(shape, lambda c: (0,) * len(shape))
    in_specs = [
        pl.BlockSpec(memory_space=pltpu.SMEM),
        field(planes, shift),
        field(2, 0),
        field(2, 0),
        fixed(flow.shape),
        fixed(second.shape),
        fixed(first.shape),
        fixed(rescale.shape),
    ]
    args = [flags, velocity, lower, upper, flow, second, first, rescale]
    out_shape = [jax.ShapeDtypeStruct(velocity.shape, jnp.bfloat16)]
    out_specs = [field(planes, shift)]
    aliases = {}
    if with_slope:
        out_shape.append(jax.ShapeDtypeStruct((planes, 2, rows, lanes), jnp.bfloat16))
        out_specs.append(pl.BlockSpec((planes, 1, rows, lanes), lambda c: (0, c, 0, 0)))
    else:
        in_specs.append(pl.BlockSpec(memory_space=pl.ANY))
        args.append(star)
        aliases = {len(args) - 1: 0}
    return pl.pallas_call(
        functools.partial(advance_kernel, with_slope),
        grid=(steps,),
        out_shape=out_shape,
        in_specs=in_specs,
        out_specs=out_specs,
        input_output_aliases=aliases,
        scratch_shapes=[
            pltpu.VMEM((planes + 4, rows, lanes), jnp.bfloat16),
            pltpu.VMEM((rows, 2 * lanes), jnp.float32),
        ],
        compiler_params=pltpu.CompilerParams(vmem_limit_bytes=VMEM_BYTES),
        cost_estimate=pl.CostEstimate(
            flops=steps * 2 * rows * rows * planes * lanes,
            bytes_accessed=steps * 4 * planes * rows * lanes,
            transcendentals=0,
        ),
        name="advance_two" if with_slope else "advance_stream",
    )(*args)


def pivot_kernel(diag, squared, pivots):
    rows = diag.shape[0]
    chunks = squared.shape[0]

    def step(j, before):
        now = 1.0 / ((2.0 + diag[j]) + squared[...] - before)
        pivots[pl.ds(pl.multiple_of(j * chunks, chunks), chunks), :] = now
        return now

    lax.fori_loop(0, rows, step, jnp.zeros_like(squared[...]))


def pivots_of(pressure_diag, squared):
    rows = pressure_diag.shape[0]
    chunks = squared.shape[0]
    return pl.pallas_call(
        pivot_kernel,
        out_shape=jax.ShapeDtypeStruct((rows * chunks, LANES), jnp.float32),
        in_specs=[pl.BlockSpec(memory_space=pltpu.SMEM), pl.BlockSpec(memory_space=pltpu.VMEM)],
        out_specs=pl.BlockSpec(memory_space=pltpu.VMEM),
        cost_estimate=pl.CostEstimate(flops=10**7, bytes_accessed=10**7, transcendentals=0),
        name="pivots",
    )(pressure_diag, squared)


def project_kernel(x, pivots, first, table, out, folded, source, high, low, part):
    blocks = x.shape[0]
    rows = x.shape[2]
    count = blocks * LANES
    half = count // 2
    tiles = count // TILE
    chunks = count // LANES
    step = pl.program_id(0)

    @pl.when(step == 0)
    def _():
        def fold(g, carry):
            for field in range(2):
                a = x[g, field].astype(jnp.float32)
                b = x[g + blocks // 2, field].astype(jnp.float32)
                at = pl.ds(pl.multiple_of(field * half + g * LANES, LANES), LANES)
                folded[0, :, at] = (a + b).astype(jnp.bfloat16)
                folded[1, :, at] = (a - b).astype(jnp.bfloat16)
            return carry

        lax.fori_loop(0, blocks // 2, fold, 0)

    @pl.when(step < tiles)
    def _():
        parity = lax.div(step, tiles // 2)
        got = jnp.dot(folded[parity], table[0], preferred_element_type=jnp.float32)
        for k in range(TILE // LANES):
            source[pl.ds(step * (TILE // LANES) + k, rows, stride=chunks), :] = got[:, k * LANES : (k + 1) * LANES]

    @pl.when(step == tiles - 1)
    def _():
        unroll = 8

        def forward(i, before):
            for k in range(unroll):
                at = pl.ds(pl.multiple_of((i * unroll + k) * chunks, chunks), chunks)
                before = pivots[at, :] * (source[at, :] + before)
                source[at, :] = before
            return before

        def backward(i, after):
            for k in range(unroll):
                j = rows - 1 - (i * unroll + k)
                at = pl.ds(pl.multiple_of(j * chunks, chunks), chunks)
                after = pivots[at, :] * after - source[at, :]
                source[at, :] = after
            return after

        zero = jnp.zeros((chunks, LANES), jnp.float32)
        lax.fori_loop(0, rows // unroll, forward, zero)
        lax.fori_loop(0, rows // unroll, backward, zero)

        for c in range(chunks):
            pressure = source[pl.ds(c, rows, stride=chunks), :]
            rounded = pressure.astype(jnp.bfloat16)
            high[:, c * LANES : (c + 1) * LANES] = rounded
            low[:, c * LANES : (c + 1) * LANES] = (pressure - rounded.astype(jnp.float32)).astype(jnp.bfloat16)

        def slopes(i, carry):
            at = pl.ds(pl.multiple_of(i * TILE, TILE), TILE)
            part[:, at] = (
                jnp.dot(first[...], high[:, at], preferred_element_type=jnp.float32)
                + jnp.dot(first[...], low[:, at], preferred_element_type=jnp.float32)
            ).astype(jnp.bfloat16)
            return carry

        lax.fori_loop(0, count // TILE, slopes, 0)

    def back(lhs, field, tile):
        even = jnp.dot(lhs[:, :half], table[0, :half], preferred_element_type=jnp.float32)
        odd = jnp.dot(lhs[:, half:], table[0, half:], preferred_element_type=jnp.float32)
        for k in range(TILE // LANES):
            at = slice(k * LANES, (k + 1) * LANES)
            g = tile * (TILE // LANES) + k
            out[g, field] = (even[:, at] + odd[:, at]).astype(jnp.bfloat16)
            out[g + blocks // 2, field] = (even[:, at] - odd[:, at]).astype(jnp.bfloat16)

    @pl.when((step >= tiles) & (step < tiles + tiles // 2))
    def _():
        back(part, 0, step - tiles)

    @pl.when(step >= tiles + tiles // 2)
    def _():
        back(high, 1, step - tiles - tiles // 2)


def project(x, pivots, wall_first, table):
    blocks, _, rows, lanes = x.shape
    count = blocks * lanes
    fixed = lambda shape: pl.BlockSpec(shape, lambda s: (0,) * len(shape))
    return pl.pallas_call(
        project_kernel,
        grid=(table.shape[0],),
        out_shape=jax.ShapeDtypeStruct(x.shape, jnp.bfloat16),
        in_specs=[
            fixed(x.shape),
            fixed(pivots.shape),
            fixed(wall_first.shape),
            pl.BlockSpec((1,) + table.shape[1:], lambda s: (s, 0, 0)),
        ],
        out_specs=fixed(x.shape),
        scratch_shapes=[
            pltpu.VMEM((2, rows, count), jnp.bfloat16),
            pltpu.VMEM((rows * count // LANES, LANES), jnp.float32),
            pltpu.VMEM((rows, count), jnp.bfloat16),
            pltpu.VMEM((rows, count), jnp.bfloat16),
            pltpu.VMEM((rows, count), jnp.bfloat16),
        ],
        compiler_params=pltpu.CompilerParams(vmem_limit_bytes=VMEM_BYTES),
        cost_estimate=pl.CostEstimate(
            flops=4 * rows * count * count, bytes_accessed=2 * table.size + 8 * x.size, transcendentals=0
        ),
        name="project",
    )(x, pivots, wall_first, table)


def correct_kernel(star, change, out):
    out[0] = (star[0].astype(jnp.float32) + change[:, 0].astype(jnp.float32)).astype(jnp.bfloat16)


def correct(star, change):
    _, planes, rows, lanes = star.shape
    group = 4
    spec = pl.BlockSpec((1, group, rows, lanes), lambda f, i: (f + 1, i, 0, 0))
    return pl.pallas_call(
        correct_kernel,
        grid=(2, planes // group),
        out_shape=jax.ShapeDtypeStruct(star.shape, jnp.bfloat16),
        in_specs=[spec, pl.BlockSpec((group, 1, rows, lanes), lambda f, i: (i, f, 0, 0))],
        out_specs=spec,
        input_output_aliases={0: 0},
        compiler_params=pltpu.CompilerParams(vmem_limit_bytes=VMEM_BYTES),
        name="correct",
    )(star, change)


def across(x):
    blocks, fields, rows, lanes = x.shape
    moved = lax.all_to_all(x.reshape(blocks, fields * rows, lanes), "gz", split_axis=0, concat_axis=0, tiled=True)
    return moved.reshape(x.shape)


def on_device(velocity, base_flow, wall_second, wall_first, rescale, pressure_diag):
    groups, slabs = lax.axis_size("grp"), lax.axis_size("gx")
    place = lax.axis_index("grp") * slabs + lax.axis_index("gx")
    ends = groups * slabs - 1
    flags = jnp.stack(
        [
            jnp.where(place == 0, 1, jnp.where(place == slabs, 2, 0)),
            jnp.where((place == slabs - 1) | (place == ends), 1, 0),
        ]
    ).astype(jnp.int32)
    up = [(i, i + 1) for i in range(ends)]
    down = [(i + 1, i) for i in range(ends)]
    lower = lax.ppermute(velocity[1:, -2:], ("grp", "gx"), up)
    upper = lax.ppermute(velocity[1:, :2], ("grp", "gx"), down)
    stream_lower = lax.ppermute(velocity[:1, -2:], ("grp", "gx"), up)
    stream_upper = lax.ppermute(velocity[:1, :2], ("grp", "gx"), down)
    flow = jnp.broadcast_to((base_flow * (step_size / 12.0))[:, None], (base_flow.shape[0], LANES))
    table, squared = (jnp.asarray(t) for t in tables(lax.axis_size("gz") * velocity.shape[3]))

    star, send = advance(flags, velocity, lower, upper, flow, wall_second, wall_first, rescale)
    pencils = across(send)
    pivots = pivots_of(pressure_diag, squared)
    (star,) = advance(flags, velocity, stream_lower, stream_upper, flow, wall_second, wall_first, rescale, star)
    change = across(project(pencils, pivots, wall_first, table))
    return correct(star, change)


def solution(mesh):
    return jax.shard_map(
        on_device,
        mesh=mesh,
        in_specs=(P(None, ("grp", "gx"), None, "gz"), P(), P(), P(), P(), P()),
        out_specs=P(None, ("grp", "gx"), None, "gz"),
        check_vma=False,
    )
```

```python
import functools
import math

import jax
import jax.numpy as jnp
import ml_dtypes
import numpy as np
from jax import lax
from jax.experimental import pallas as pl
from jax.experimental.pallas import tpu as pltpu
from jax.sharding import PartitionSpec as P

step_size = 0.25
viscosity = 0.4
LANES = 128
TILE = 256
ALL_BYTES = 62914560
MOST_BYTES = 51000000
LAST_BYTES = 53000000
EDGE_BYTES = 54500000
PIVOT_SPACE = 6
SMALL_BYTES = 12 * 1024 * 1024


def mode_columns(count):
    quarter = count // 4
    even = 2 * np.arange(quarter)
    odd = even + 1
    sine_even = even.copy()
    sine_even[0] = count // 2
    is_sine = np.concatenate([np.zeros(quarter), np.ones(quarter), np.zeros(quarter), np.ones(quarter)]).astype(bool)
    is_sine[quarter] = False
    return np.concatenate([even, sine_even, odd, odd]).astype(np.int64), is_sine


@functools.lru_cache(maxsize=None)
def tables(count):
    half = count // 2
    mode, is_sine = mode_columns(count)
    z = np.arange(half, dtype=np.int64)
    angle = (z[:, None] * mode[None, :] % count).astype(np.float64) * (2.0 * math.pi / count)
    cosine, sine = np.cos(angle), np.sin(angle)
    own = np.where(is_sine[None, :], sine, cosine) / math.sqrt(count)
    signed = np.where((mode == 0) | (mode == half), 0, mode) * (2.0 * math.pi / count)
    other = np.where(is_sine[None, :], cosine, -sine) * signed[None, :] / math.sqrt(count)
    weight = np.where((mode == 0) | (mode == half), 1.0, 2.0)
    to_modes = [own / step_size, -other / step_size]
    from_modes = [-step_size * own * weight, -step_size * other * weight]
    steps = []
    for start in range(0, count, TILE):
        steps.append(np.concatenate([t[:, start : start + TILE] for t in to_modes], 0))
    for table in from_modes:
        for start in range(0, half, TILE):
            steps.append(
                np.concatenate([table[start : start + TILE, :half].T, table[start : start + TILE, half:].T], 0)
            )
    folded = np.minimum(mode, count - mode).astype(np.float64) * (2.0 * math.pi / count)
    return (
        np.stack(steps).astype(np.float32).astype(ml_dtypes.bfloat16),
        (folded * folded).astype(np.float32).reshape(count // LANES, LANES),
    )


def provisional(pad, at, field, flow, second, acc, store):
    rows = second.shape[0]
    strip = 80
    bend_scale = step_size * viscosity / 12.0
    normal_scale = step_size * viscosity
    both = jnp.concatenate([pad(field, at), pad(field, at + 1)], 1)
    acc[...] = jnp.dot(second[...], both, preferred_element_type=jnp.float32)
    for row in range(0, rows, strip):
        here = pl.ds(row, strip)
        ghost = [pad(field, at + k - 2, here).astype(jnp.float32) for k in range(6)]
        for half in range(2):
            far_low, low, centre, high, far_high = ghost[half : half + 5]
            bend = 16.0 * (low + high) - (far_low + far_high) - 30.0 * centre
            slope = 8.0 * (high - low) - (far_high - far_low)
            new = (
                centre
                + normal_scale * acc[here, half * LANES : (half + 1) * LANES]
                + bend_scale * bend
                - flow[here, :] * slope
            )
            store(field, at + half, here, new.astype(jnp.bfloat16))


def slope_pair(first, star, send, at):
    both = jnp.concatenate([star[0, at], star[0, at + 1]], 1)
    out = jnp.dot(first[...], both, preferred_element_type=jnp.float32).astype(jnp.bfloat16)
    send[at, 0] = out[:, :LANES]
    send[at + 1, 0] = out[:, LANES:]


def inner_kernel(velocity, flow, second, first, star_out, send_out, vel, star, send, acc, loads, sems):
    planes = vel.shape[1]

    def load(i):
        here = pl.ds(2 * i, 2)
        return pltpu.make_async_copy(velocity.at[pl.ds(1, 2), here], vel.at[:, here], loads.at[i])

    for i in range(planes // 2):
        load(i).start()

    def pad(field, plane, here=slice(None)):
        return vel[field, plane, here, :]

    def store(field, plane, here, value):
        star[field, plane, here, :] = value
        if field == 1:
            send[plane, 1, here, :] = value

    def copies(i):
        here = pl.ds(2 * i, 2)
        return (
            pltpu.make_async_copy(send.at[here], send_out.at[here], sems.at[0, i]),
            pltpu.make_async_copy(star.at[:, here], star_out.at[:, here], sems.at[1, i]),
        )

    def pair(i, carry):
        load(i + 1).wait()
        for field in range(2):
            provisional(pad, 2 * i, field, flow, second, acc, store)
        slope_pair(first, star, send, 2 * i)
        for copy in copies(i):
            copy.start()
        return carry

    def settle(i, carry):
        for copy in copies(i):
            copy.wait()
        return carry

    load(0).wait()
    load(1).wait()
    lax.fori_loop(1, planes // 2 - 1, pair, 0)
    lax.fori_loop(1, planes // 2 - 1, settle, 0)


def rim_loads(velocity, fields, planes, lower, upper, rim, sems):
    return [
        pltpu.make_async_copy(velocity.at[fields, pl.ds(0, 4)], rim.at[:, 0, pl.ds(2, 4)], sems.at[0]),
        pltpu.make_async_copy(velocity.at[fields, pl.ds(planes - 4, 4)], rim.at[:, 1, pl.ds(0, 4)], sems.at[1]),
        pltpu.make_async_copy(lower, rim.at[:, 0, pl.ds(0, 2)], sems.at[2]),
        pltpu.make_async_copy(upper, rim.at[:, 1, pl.ds(4, 2)], sems.at[3]),
    ]


def fix_rims(flags, rescale, rim):
    fields = rim.shape[0]

    @pl.when(flags[0] == 1)
    def _():
        for field in range(fields):
            rim[field, 0, 0] = rim[field, 0, 2]
            rim[field, 0, 1] = rim[field, 0, 2]

    @pl.when(flags[0] == 2)
    def _():
        for field in range(fields):
            both = jnp.concatenate([rim[field, 0, 0], rim[field, 0, 1]], 1)
            inflow = jnp.dot(rescale[...], both, preferred_element_type=jnp.float32).astype(jnp.bfloat16)
            rim[field, 0, 0] = inflow[:, :LANES]
            rim[field, 0, 1] = inflow[:, LANES:]

    @pl.when(flags[1] == 1)
    def _():
        for field in range(fields):
            rim[field, 1, 4] = rim[field, 1, 3]
            rim[field, 1, 5] = rim[field, 1, 3]


def outer_kernel(
    flags, velocity, lower, upper, flow, second, first, rescale, star_in, send_in, star, send, rim, edge, away, acc, loads, sems
):
    planes = velocity.shape[1]
    arrive = rim_loads(velocity, pl.ds(1, 2), planes, lower, upper, rim, loads)
    for copy in arrive:
        copy.start()
    for copy in arrive:
        copy.wait()
    fix_rims(flags, rescale, rim)
    copies = []
    for side in range(2):
        base = 2 * side

        def pad(field, plane, here=slice(None)):
            return rim[field, side, plane - base + 2, here, :]

        def store(field, plane, here, value):
            edge[field, plane, here, :] = value
            if field == 1:
                away[plane, 1, here, :] = value

        for field in range(2):
            provisional(pad, base, field, flow, second, acc, store)
        slope_pair(first, edge, away, base)
        here, there = pl.ds(base, 2), pl.ds(0 if side == 0 else planes - 2, 2)
        for source, target in ((away.at[here], send.at[there]), (edge.at[:, here], star.at[:, there])):
            copies.append(pltpu.make_async_copy(source, target, sems.at[len(copies)]))
            copies[-1].start()
    for copy in copies:
        copy.wait()


def stream_kernel(flags, velocity, lower, upper, flow, second, rescale, result, vel, rim, star, acc, loads, sems):
    planes = velocity.shape[1]
    arrive = rim_loads(velocity, pl.ds(0, 1), planes, lower, upper, rim, loads)
    arrive.append(pltpu.make_async_copy(velocity.at[0], vel, loads.at[4]))
    for copy in arrive:
        copy.start()
    for copy in arrive:
        copy.wait()
    fix_rims(flags, rescale, rim)

    def store(field, plane, here, value):
        star[plane, here, :] = value

    def pad(field, plane, here=slice(None)):
        return vel[plane, here, :]

    def copy(i):
        here = pl.ds(2 * i, 2)
        return pltpu.make_async_copy(star.at[here], result.at[0, here], sems.at[i])

    def pair(i, carry):
        provisional(pad, 2 * i, 0, flow, second, acc, store)
        copy(i).start()
        return carry

    def settle(i, carry):
        copy(i).wait()
        return carry

    lax.fori_loop(1, planes // 2 - 1, pair, 0)
    for side in range(2):
        base = 0 if side == 0 else planes - 2

        def rim_pad(field, plane, here=slice(None)):
            return rim[field, side, plane - base + 2, here, :]

        provisional(rim_pad, base, 0, flow, second, acc, store)
        copy(base // 2).start()
    lax.fori_loop(0, planes // 2, settle, 0)


in_vmem = pl.BlockSpec(memory_space=pltpu.VMEM)
in_smem = pl.BlockSpec(memory_space=pltpu.SMEM)
in_hbm = pl.BlockSpec(memory_space=pltpu.HBM)


def cost_of(fields, planes, rows, lanes):
    return pl.CostEstimate(
        flops=fields * planes * rows * lanes * 2 * rows, bytes_accessed=4 * fields * planes * rows * lanes, transcendentals=0
    )


def advance_inner(velocity, flow, second, first):
    _, planes, rows, lanes = velocity.shape
    return pl.pallas_call(
        inner_kernel,
        out_shape=[
            jax.ShapeDtypeStruct((2, planes, rows, lanes), jnp.bfloat16),
            jax.ShapeDtypeStruct((planes, 2, rows, lanes), jnp.bfloat16),
        ],
        in_specs=[in_hbm] + [in_vmem] * 3,
        out_specs=[in_hbm] * 2,
        scratch_shapes=[
            pltpu.VMEM((2, planes, rows, lanes), jnp.bfloat16),
            pltpu.VMEM((2, planes, rows, lanes), jnp.bfloat16),
            pltpu.VMEM((planes, 2, rows, lanes), jnp.bfloat16),
            pltpu.VMEM((rows, 2 * lanes), jnp.float32),
            pltpu.SemaphoreType.DMA((planes // 2,)),
            pltpu.SemaphoreType.DMA((2, planes // 2)),
        ],
        compiler_params=pltpu.CompilerParams(vmem_limit_bytes=EDGE_BYTES),
        cost_estimate=cost_of(2, planes, rows, lanes),
        name="advance_inner",
    )(velocity, flow, second, first)


def advance_outer(flags, velocity, lower, upper, flow, second, first, rescale, star, send):
    _, planes, rows, lanes = velocity.shape
    return pl.pallas_call(
        outer_kernel,
        out_shape=[
            jax.ShapeDtypeStruct(star.shape, jnp.bfloat16),
            jax.ShapeDtypeStruct(send.shape, jnp.bfloat16),
        ],
        in_specs=[in_smem] + [in_hbm] * 3 + [in_vmem] * 4 + [in_hbm] * 2,
        out_specs=[in_hbm] * 2,
        input_output_aliases={8: 0, 9: 1},
        scratch_shapes=[
            pltpu.VMEM((2, 2, 6, rows, lanes), jnp.bfloat16),
            pltpu.VMEM((2, 4, rows, lanes), jnp.bfloat16),
            pltpu.VMEM((4, 2, rows, lanes), jnp.bfloat16),
            pltpu.VMEM((rows, 2 * lanes), jnp.float32),
            pltpu.SemaphoreType.DMA((4,)),
            pltpu.SemaphoreType.DMA((4,)),
        ],
        compiler_params=pltpu.CompilerParams(vmem_limit_bytes=EDGE_BYTES),
        cost_estimate=cost_of(2, 4, rows, lanes),
        name="advance_outer",
    )(flags, velocity, lower, upper, flow, second, first, rescale, star, send)


def advance_stream(flags, velocity, lower, upper, flow, second, rescale):
    _, planes, rows, lanes = velocity.shape
    return pl.pallas_call(
        stream_kernel,
        out_shape=jax.ShapeDtypeStruct(velocity.shape, jnp.bfloat16),
        in_specs=[in_smem] + [in_hbm] * 3 + [in_vmem] * 3,
        out_specs=in_hbm,
        scratch_shapes=[
            pltpu.VMEM((planes, rows, lanes), jnp.bfloat16),
            pltpu.VMEM((1, 2, 6, rows, lanes), jnp.bfloat16),
            pltpu.VMEM((planes, rows, lanes), jnp.bfloat16),
            pltpu.VMEM((rows, 2 * lanes), jnp.float32),
            pltpu.SemaphoreType.DMA((5,)),
            pltpu.SemaphoreType.DMA((planes // 2,)),
        ],
        compiler_params=pltpu.CompilerParams(vmem_limit_bytes=EDGE_BYTES),
        cost_estimate=cost_of(1, planes, rows, lanes),
        name="advance_stream",
    )(flags, velocity, lower, upper, flow, second, rescale)


def pivot_kernel(diag, squared, out, pivots, sem):
    rows = diag.shape[0]
    chunks = squared.shape[0]

    def step(j, before):
        now = 1.0 / ((2.0 + diag[j]) + squared[...] - before)
        pivots[pl.ds(pl.multiple_of(j * chunks, chunks), chunks), :] = now
        return now

    lax.fori_loop(0, rows, step, jnp.zeros_like(squared[...]))
    copy = pltpu.make_async_copy(pivots, out.at[pl.ds(0, rows * chunks)], sem)
    copy.start()
    copy.wait()


def pivots_of(pressure_diag, squared):
    rows = pressure_diag.shape[0]
    chunks = squared.shape[0]
    return pl.pallas_call(
        pivot_kernel,
        out_shape=jax.ShapeDtypeStruct((PIVOT_SPACE * rows * chunks, LANES), jnp.float32),
        in_specs=[in_smem, in_vmem],
        out_specs=in_hbm,
        scratch_shapes=[pltpu.VMEM((rows * chunks, LANES), jnp.float32), pltpu.SemaphoreType.DMA],
        compiler_params=pltpu.CompilerParams(vmem_limit_bytes=ALL_BYTES),
        cost_estimate=pl.CostEstimate(flops=10**7, bytes_accessed=10**7, transcendentals=0),
        name="pivots",
    )(pressure_diag, squared)


def project_kernel(
    x, pivots_in, first, table_in, out, table, pivots, ready, folded, source, high, low, part, table_sems, pivot_sem, out_sems
):
    blocks, _, rows, _ = x.shape
    count = blocks * LANES
    half = count // 2
    tiles = count // TILE
    chunks = count // LANES
    per = TILE // LANES

    def load(i):
        return pltpu.make_async_copy(table_in.at[i], table.at[i], table_sems.at[i])

    load_pivots = pltpu.make_async_copy(pivots_in.at[pl.ds(0, rows * chunks)], pivots, pivot_sem)
    for i in range(2 * tiles):
        load(i).start()
        if i == tiles // 2:
            load_pivots.start()

    def fold(g, carry):
        for field in range(2):
            a = x[g, field].astype(jnp.float32)
            b = x[g + blocks // 2, field].astype(jnp.float32)
            at = pl.ds(pl.multiple_of(field * half + g * LANES, LANES), LANES)
            folded[0, :, at] = (a + b).astype(jnp.bfloat16)
            folded[1, :, at] = (a - b).astype(jnp.bfloat16)
        return carry

    lax.fori_loop(0, blocks // 2, fold, 0)

    def to_modes(step, carry):
        load(step).wait()
        got = jnp.dot(folded[lax.div(step, tiles // 2)], table[step], preferred_element_type=jnp.float32)
        for k in range(per):
            source[pl.ds(step * per + k, rows, stride=chunks), :] = got[:, k * LANES : (k + 1) * LANES]
        return carry

    lax.fori_loop(0, tiles, to_modes, 0)

    load_pivots.wait()
    unroll = 8

    def forward(i, before):
        for k in range(unroll):
            at = pl.ds(pl.multiple_of((i * unroll + k) * chunks, chunks), chunks)
            before = pivots[at, :] * (source[at, :] + before)
            source[at, :] = before
        return before

    def backward(i, after):
        for k in range(unroll):
            j = rows - 1 - (i * unroll + k)
            at = pl.ds(pl.multiple_of(j * chunks, chunks), chunks)
            after = pivots[at, :] * after - source[at, :]
            source[at, :] = after
        return after

    zero = jnp.zeros((chunks, LANES), jnp.float32)
    lax.fori_loop(0, rows // unroll, forward, zero)
    lax.fori_loop(0, rows // unroll, backward, zero)

    def slopes(i, carry):
        for k in range(per):
            pressure = source[pl.ds(i * per + k, rows, stride=chunks), :]
            rounded = pressure.astype(jnp.bfloat16)
            at = pl.ds(pl.multiple_of((i * per + k) * LANES, LANES), LANES)
            high[:, at] = rounded
            low[:, k * LANES : (k + 1) * LANES] = (pressure - rounded.astype(jnp.float32)).astype(jnp.bfloat16)
        at = pl.ds(pl.multiple_of(i * TILE, TILE), TILE)
        part[:, at] = (
            jnp.dot(first[...], high[:, at], preferred_element_type=jnp.float32)
            + jnp.dot(first[...], low[...], preferred_element_type=jnp.float32)
        ).astype(jnp.bfloat16)
        return carry

    lax.fori_loop(0, tiles, slopes, 0)

    def leave(g, field):
        return pltpu.make_async_copy(ready.at[g, field], out.at[g, field], out_sems.at[g, field])

    for field, lhs in ((1, high), (0, part)):

        def from_modes(tile, carry):
            step = tiles + field * (tiles // 2) + tile
            load(step).wait()
            even = jnp.dot(lhs[:, :half], table[step, :half], preferred_element_type=jnp.float32)
            odd = jnp.dot(lhs[:, half:], table[step, half:], preferred_element_type=jnp.float32)
            for k in range(per):
                at = slice(k * LANES, (k + 1) * LANES)
                g = tile * per + k
                ready[g, field] = (even[:, at] + odd[:, at]).astype(jnp.bfloat16)
                leave(g, field).start()
                ready[g + blocks // 2, field] = (even[:, at] - odd[:, at]).astype(jnp.bfloat16)
                leave(g + blocks // 2, field).start()
            return carry

        lax.fori_loop(0, tiles // 2, from_modes, 0)

    def settle(g, carry):
        for field in range(2):
            leave(g, field).wait()
        return carry

    lax.fori_loop(0, blocks, settle, 0)


def project(x, pivots, wall_first, table):
    blocks, _, rows, lanes = x.shape
    count = blocks * lanes
    return pl.pallas_call(
        project_kernel,
        out_shape=jax.ShapeDtypeStruct(x.shape, jnp.bfloat16),
        in_specs=[in_vmem, in_hbm, in_vmem, in_hbm],
        out_specs=in_hbm,
        scratch_shapes=[
            pltpu.VMEM(table.shape, jnp.bfloat16),
            pltpu.VMEM((rows * count // LANES, LANES), jnp.float32),
            pltpu.VMEM(x.shape, jnp.bfloat16),
            pltpu.VMEM((2, rows, count), jnp.bfloat16),
            pltpu.VMEM((rows * count // LANES, LANES), jnp.float32),
            pltpu.VMEM((rows, count), jnp.bfloat16),
            pltpu.VMEM((rows, TILE), jnp.bfloat16),
            pltpu.VMEM((rows, count), jnp.bfloat16),
            pltpu.SemaphoreType.DMA((table.shape[0],)),
            pltpu.SemaphoreType.DMA,
            pltpu.SemaphoreType.DMA((blocks, 2)),
        ],
        compiler_params=pltpu.CompilerParams(vmem_limit_bytes=MOST_BYTES),
        cost_estimate=pl.CostEstimate(
            flops=4 * rows * count * count, bytes_accessed=2 * table.size + 8 * x.size, transcendentals=0
        ),
        name="project",
    )(x, pivots, wall_first, table)


def correct_kernel(result_in, star, change_in, result, change, ready, loads, sems):
    planes = star.shape[1]
    group = 4
    pieces = [(field, pl.ds(start, group)) for start in range(0, planes, group) for field in range(2)]
    arrive = [
        pltpu.make_async_copy(change_in.at[pl.ds(start, group)], change.at[pl.ds(start, group)], loads.at[start // group])
        for start in range(0, planes, group)
    ]
    depart = [
        pltpu.make_async_copy(ready.at[field, here], result.at[field + 1, here], sems.at[i])
        for i, (field, here) in enumerate(pieces)
    ]
    for copy in arrive:
        copy.start()
    for i, (field, here) in enumerate(pieces):
        if field == 0:
            arrive[i // 2].wait()
        ready[field, here] = (
            star[field, here].astype(jnp.float32) + change[here, field].astype(jnp.float32)
        ).astype(jnp.bfloat16)
        depart[i].start()
    for copy in depart:
        copy.wait()


def correct(result, star, change):
    planes = star.shape[1]
    return pl.pallas_call(
        correct_kernel,
        out_shape=jax.ShapeDtypeStruct(result.shape, jnp.bfloat16),
        in_specs=[in_hbm, in_vmem, in_hbm],
        out_specs=in_hbm,
        input_output_aliases={0: 0},
        scratch_shapes=[
            pltpu.VMEM(change.shape, jnp.bfloat16),
            pltpu.VMEM(star.shape, jnp.bfloat16),
            pltpu.SemaphoreType.DMA((planes // 4,)),
            pltpu.SemaphoreType.DMA((2 * planes // 4,)),
        ],
        compiler_params=pltpu.CompilerParams(vmem_limit_bytes=LAST_BYTES),
        name="correct",
    )(result, star, change)


def across(x):
    blocks, fields, rows, lanes = x.shape
    moved = lax.all_to_all(x.reshape(blocks, fields * rows, lanes), "gz", split_axis=0, concat_axis=0, tiled=True)
    return moved.reshape(x.shape)


def on_device(velocity, base_flow, wall_second, wall_first, rescale, pressure_diag):
    groups, slabs = lax.axis_size("grp"), lax.axis_size("gx")
    place = lax.axis_index("grp") * slabs + lax.axis_index("gx")
    ends = groups * slabs - 1
    flags = jnp.stack(
        [
            jnp.where(place == 0, 1, jnp.where(place == slabs, 2, 0)),
            jnp.where((place == slabs - 1) | (place == ends), 1, 0),
        ]
    ).astype(jnp.int32)
    up = [(i, i + 1) for i in range(ends)]
    down = [(i + 1, i) for i in range(ends)]
    lower = lax.ppermute(velocity[1:, -2:], ("grp", "gx"), up)
    upper = lax.ppermute(velocity[1:, :2], ("grp", "gx"), down)
    stream_lower = lax.ppermute(velocity[:1, -2:], ("grp", "gx"), up)
    stream_upper = lax.ppermute(velocity[:1, :2], ("grp", "gx"), down)
    flow = jnp.broadcast_to((base_flow * (step_size / 12.0))[:, None], (base_flow.shape[0], LANES))
    table, squared = (jnp.asarray(t) for t in tables(lax.axis_size("gz") * velocity.shape[3]))

    star, send = advance_inner(velocity, flow, wall_second, wall_first)
    star, send = advance_outer(flags, velocity, lower, upper, flow, wall_second, wall_first, rescale, star, send)
    pencils = across(send)
    pivots = pivots_of(pressure_diag, squared)
    result = advance_stream(flags, velocity, stream_lower, stream_upper, flow, wall_second, rescale)
    change = across(project(pencils, pivots, wall_first, table))
    return correct(result, star, change)


def solution(mesh):
    return jax.shard_map(
        on_device,
        mesh=mesh,
        in_specs=(P(None, ("grp", "gx"), None, "gz"), P(), P(), P(), P(), P()),
        out_specs=P(None, ("grp", "gx"), None, "gz"),
        check_vma=False,
    )
```

```python
import functools
import math

import jax
import jax.numpy as jnp
import ml_dtypes
import numpy as np
from jax import lax
from jax.experimental import pallas as pl
from jax.experimental.pallas import tpu as pltpu
from jax.sharding import PartitionSpec as P

step_size = 0.25
viscosity = 0.4
LANES = 128
TILE = 256
ALL_BYTES = 62914560
MOST_BYTES = 51000000
LAST_BYTES = 53000000
EDGE_BYTES = 54500000
PIVOT_SPACE = 6
SMALL_BYTES = 12 * 1024 * 1024


def mode_columns(count):
    quarter = count // 4
    even = 2 * np.arange(quarter)
    odd = even + 1
    sine_even = even.copy()
    sine_even[0] = count // 2
    is_sine = np.concatenate([np.zeros(quarter), np.ones(quarter), np.zeros(quarter), np.ones(quarter)]).astype(bool)
    is_sine[quarter] = False
    return np.concatenate([even, sine_even, odd, odd]).astype(np.int64), is_sine


@functools.lru_cache(maxsize=None)
def tables(count):
    half = count // 2
    mode, is_sine = mode_columns(count)
    z = np.arange(half, dtype=np.int64)
    angle = (z[:, None] * mode[None, :] % count).astype(np.float64) * (2.0 * math.pi / count)
    cosine, sine = np.cos(angle), np.sin(angle)
    own = np.where(is_sine[None, :], sine, cosine) / math.sqrt(count)
    signed = np.where((mode == 0) | (mode == half), 0, mode) * (2.0 * math.pi / count)
    weight = np.where((mode == 0) | (mode == half), 1.0, 2.0)
    cosines = np.concatenate([np.arange(count // 4), half + np.arange(count // 4)])
    waves = signed[cosines].reshape(-1, TILE)
    to_modes = [own[:, start : start + TILE] for start in range(0, count, TILE)]
    back = -step_size * own * weight
    from_modes = [
        np.concatenate([back[start : start + TILE, :half].T, back[start : start + TILE, half:].T], 0)
        for start in range(0, half, TILE)
    ]
    folded = np.minimum(mode, count - mode).astype(np.float64) * (2.0 * math.pi / count)
    return (
        np.stack(to_modes).astype(np.float32).astype(ml_dtypes.bfloat16),
        np.stack(from_modes).astype(np.float32).astype(ml_dtypes.bfloat16),
        waves.astype(np.float32),
        (folded * folded).astype(np.float32).reshape(count // LANES, LANES),
    )


def provisional(pad, at, field, flow, second, acc, store):
    rows = second.shape[0]
    strip = 80
    bend_scale = step_size * viscosity / 12.0
    normal_scale = step_size * viscosity
    both = jnp.concatenate([pad(field, at), pad(field, at + 1)], 1)
    acc[...] = jnp.dot(second[...], both, preferred_element_type=jnp.float32)
    for row in range(0, rows, strip):
        here = pl.ds(row, strip)
        ghost = [pad(field, at + k - 2, here).astype(jnp.float32) for k in range(6)]
        for half in range(2):
            far_low, low, centre, high, far_high = ghost[half : half + 5]
            bend = 16.0 * (low + high) - (far_low + far_high) - 30.0 * centre
            slope = 8.0 * (high - low) - (far_high - far_low)
            new = (
                centre
                + normal_scale * acc[here, half * LANES : (half + 1) * LANES]
                + bend_scale * bend
                - flow[here, :] * slope
            )
            store(field, at + half, here, new.astype(jnp.bfloat16))


def slope_pair(first, star, send, at):
    both = jnp.concatenate([star[0, at], star[0, at + 1]], 1)
    out = jnp.dot(first[...], both, preferred_element_type=jnp.float32).astype(jnp.bfloat16)
    send[at, 0] = out[:, :LANES]
    send[at + 1, 0] = out[:, LANES:]


def inner_kernel(
    velocity, flow_in, second_in, first_in, star_out, send_out, vel, star, send, acc, flow, second, first, loads, fixed_sems, sems
):
    planes = vel.shape[1]
    fixed = [
        pltpu.make_async_copy(source, target, fixed_sems.at[i])
        for i, (source, target) in enumerate(((second_in, second), (flow_in, flow), (first_in, first)))
    ]
    for copy in fixed:
        copy.start()

    def load(i):
        here = pl.ds(2 * i, 2)
        return pltpu.make_async_copy(velocity.at[pl.ds(1, 2), here], vel.at[:, here], loads.at[i])

    for i in range(planes // 2):
        load(i).start()

    def pad(field, plane, here=slice(None)):
        return vel[field, plane, here, :]

    def store(field, plane, here, value):
        star[field, plane, here, :] = value
        if field == 1:
            send[plane, 1, here, :] = value

    def copies(i):
        here = pl.ds(2 * i, 2)
        return (
            pltpu.make_async_copy(send.at[here], send_out.at[here], sems.at[0, i]),
            pltpu.make_async_copy(star.at[:, here], star_out.at[:, here], sems.at[1, i]),
        )

    def pair(i, carry):
        load(i + 1).wait()
        for field in range(2):
            provisional(pad, 2 * i, field, flow, second, acc, store)
        slope_pair(first, star, send, 2 * i)
        for copy in copies(i):
            copy.start()
        return carry

    def settle(i, carry):
        for copy in copies(i):
            copy.wait()
        return carry

    for copy in fixed:
        copy.wait()
    load(0).wait()
    load(1).wait()
    lax.fori_loop(1, planes // 2 - 1, pair, 0)
    lax.fori_loop(1, planes // 2 - 1, settle, 0)


def rim_loads(velocity, fields, planes, lower, upper, rim, sems):
    return [
        pltpu.make_async_copy(velocity.at[fields, pl.ds(0, 4)], rim.at[:, 0, pl.ds(2, 4)], sems.at[0]),
        pltpu.make_async_copy(velocity.at[fields, pl.ds(planes - 4, 4)], rim.at[:, 1, pl.ds(0, 4)], sems.at[1]),
        pltpu.make_async_copy(lower, rim.at[:, 0, pl.ds(0, 2)], sems.at[2]),
        pltpu.make_async_copy(upper, rim.at[:, 1, pl.ds(4, 2)], sems.at[3]),
    ]


def fix_rims(flags, rescale, rim):
    fields = rim.shape[0]

    @pl.when(flags[0] == 1)
    def _():
        for field in range(fields):
            rim[field, 0, 0] = rim[field, 0, 2]
            rim[field, 0, 1] = rim[field, 0, 2]

    @pl.when(flags[0] == 2)
    def _():
        for field in range(fields):
            both = jnp.concatenate([rim[field, 0, 0], rim[field, 0, 1]], 1)
            inflow = jnp.dot(rescale[...], both, preferred_element_type=jnp.float32).astype(jnp.bfloat16)
            rim[field, 0, 0] = inflow[:, :LANES]
            rim[field, 0, 1] = inflow[:, LANES:]

    @pl.when(flags[1] == 1)
    def _():
        for field in range(fields):
            rim[field, 1, 4] = rim[field, 1, 3]
            rim[field, 1, 5] = rim[field, 1, 3]


def outer_kernel(
    flags, velocity, lower, upper, flow, second, first, rescale, star_in, send_in, star, send, rim, edge, away, acc, loads, sems
):
    planes = velocity.shape[1]
    arrive = rim_loads(velocity, pl.ds(1, 2), planes, lower, upper, rim, loads)
    for copy in arrive:
        copy.start()
    for copy in arrive:
        copy.wait()
    fix_rims(flags, rescale, rim)
    copies = []
    for side in range(2):
        base = 2 * side

        def pad(field, plane, here=slice(None)):
            return rim[field, side, plane - base + 2, here, :]

        def store(field, plane, here, value):
            edge[field, plane, here, :] = value
            if field == 1:
                away[plane, 1, here, :] = value

        for field in range(2):
            provisional(pad, base, field, flow, second, acc, store)
        slope_pair(first, edge, away, base)
        here, there = pl.ds(base, 2), pl.ds(0 if side == 0 else planes - 2, 2)
        for source, target in ((away.at[here], send.at[there]), (edge.at[:, here], star.at[:, there])):
            copies.append(pltpu.make_async_copy(source, target, sems.at[len(copies)]))
            copies[-1].start()
    for copy in copies:
        copy.wait()


def stream_kernel(flags, velocity, lower, upper, flow, second, rescale, result, vel, rim, star, acc, loads, sems):
    planes = velocity.shape[1]
    arrive = rim_loads(velocity, pl.ds(0, 1), planes, lower, upper, rim, loads)
    arrive.append(pltpu.make_async_copy(velocity.at[0], vel, loads.at[4]))
    for copy in arrive:
        copy.start()
    for copy in arrive:
        copy.wait()
    fix_rims(flags, rescale, rim)

    def store(field, plane, here, value):
        star[plane, here, :] = value

    def pad(field, plane, here=slice(None)):
        return vel[plane, here, :]

    def copy(i):
        here = pl.ds(2 * i, 2)
        return pltpu.make_async_copy(star.at[here], result.at[0, here], sems.at[i])

    def pair(i, carry):
        provisional(pad, 2 * i, 0, flow, second, acc, store)
        copy(i).start()
        return carry

    def settle(i, carry):
        copy(i).wait()
        return carry

    lax.fori_loop(1, planes // 2 - 1, pair, 0)
    for side in range(2):
        base = 0 if side == 0 else planes - 2

        def rim_pad(field, plane, here=slice(None)):
            return rim[field, side, plane - base + 2, here, :]

        provisional(rim_pad, base, 0, flow, second, acc, store)
        copy(base // 2).start()
    lax.fori_loop(0, planes // 2, settle, 0)


in_vmem = pl.BlockSpec(memory_space=pltpu.VMEM)
in_smem = pl.BlockSpec(memory_space=pltpu.SMEM)
in_hbm = pl.BlockSpec(memory_space=pltpu.HBM)


def cost_of(fields, planes, rows, lanes):
    return pl.CostEstimate(
        flops=fields * planes * rows * lanes * 2 * rows, bytes_accessed=4 * fields * planes * rows * lanes, transcendentals=0
    )


def advance_inner(velocity, flow, second, first):
    _, planes, rows, lanes = velocity.shape
    return pl.pallas_call(
        inner_kernel,
        out_shape=[
            jax.ShapeDtypeStruct((2, planes, rows, lanes), jnp.bfloat16),
            jax.ShapeDtypeStruct((planes, 2, rows, lanes), jnp.bfloat16),
        ],
        in_specs=[in_hbm] * 4,
        out_specs=[in_hbm] * 2,
        scratch_shapes=[
            pltpu.VMEM((2, planes, rows, lanes), jnp.bfloat16),
            pltpu.VMEM((2, planes, rows, lanes), jnp.bfloat16),
            pltpu.VMEM((planes, 2, rows, lanes), jnp.bfloat16),
            pltpu.VMEM((rows, 2 * lanes), jnp.float32),
            pltpu.VMEM(flow.shape, jnp.float32),
            pltpu.VMEM(second.shape, jnp.bfloat16),
            pltpu.VMEM(first.shape, jnp.bfloat16),
            pltpu.SemaphoreType.DMA((planes // 2,)),
            pltpu.SemaphoreType.DMA((3,)),
            pltpu.SemaphoreType.DMA((2, planes // 2)),
        ],
        compiler_params=pltpu.CompilerParams(vmem_limit_bytes=ALL_BYTES),
        cost_estimate=cost_of(2, planes, rows, lanes),
        name="advance_inner",
    )(velocity, flow, second, first)


def advance_outer(flags, velocity, lower, upper, flow, second, first, rescale, star, send):
    _, planes, rows, lanes = velocity.shape
    return pl.pallas_call(
        outer_kernel,
        out_shape=[
            jax.ShapeDtypeStruct(star.shape, jnp.bfloat16),
            jax.ShapeDtypeStruct(send.shape, jnp.bfloat16),
        ],
        in_specs=[in_smem] + [in_hbm] * 3 + [in_vmem] * 4 + [in_hbm] * 2,
        out_specs=[in_hbm] * 2,
        input_output_aliases={8: 0, 9: 1},
        scratch_shapes=[
            pltpu.VMEM((2, 2, 6, rows, lanes), jnp.bfloat16),
            pltpu.VMEM((2, 4, rows, lanes), jnp.bfloat16),
            pltpu.VMEM((4, 2, rows, lanes), jnp.bfloat16),
            pltpu.VMEM((rows, 2 * lanes), jnp.float32),
            pltpu.SemaphoreType.DMA((4,)),
            pltpu.SemaphoreType.DMA((4,)),
        ],
        compiler_params=pltpu.CompilerParams(vmem_limit_bytes=EDGE_BYTES),
        cost_estimate=cost_of(2, 4, rows, lanes),
        name="advance_outer",
    )(flags, velocity, lower, upper, flow, second, first, rescale, star, send)


def advance_stream(flags, velocity, lower, upper, flow, second, rescale):
    _, planes, rows, lanes = velocity.shape
    return pl.pallas_call(
        stream_kernel,
        out_shape=jax.ShapeDtypeStruct(velocity.shape, jnp.bfloat16),
        in_specs=[in_smem] + [in_hbm] * 3 + [in_vmem] * 3,
        out_specs=in_hbm,
        scratch_shapes=[
            pltpu.VMEM((planes, rows, lanes), jnp.bfloat16),
            pltpu.VMEM((1, 2, 6, rows, lanes), jnp.bfloat16),
            pltpu.VMEM((planes, rows, lanes), jnp.bfloat16),
            pltpu.VMEM((rows, 2 * lanes), jnp.float32),
            pltpu.SemaphoreType.DMA((5,)),
            pltpu.SemaphoreType.DMA((planes // 2,)),
        ],
        compiler_params=pltpu.CompilerParams(vmem_limit_bytes=EDGE_BYTES),
        cost_estimate=cost_of(1, planes, rows, lanes),
        name="advance_stream",
    )(flags, velocity, lower, upper, flow, second, rescale)


def pivot_kernel(diag, squared, out, pivots, sem):
    rows = diag.shape[0]
    chunks = squared.shape[0]

    def step(j, before):
        now = 1.0 / ((2.0 + diag[j]) + squared[...] - before)
        pivots[pl.ds(pl.multiple_of(j * chunks, chunks), chunks), :] = now
        return now

    lax.fori_loop(0, rows, step, jnp.zeros_like(squared[...]))
    copy = pltpu.make_async_copy(pivots, out.at[pl.ds(0, rows * chunks)], sem)
    copy.start()
    copy.wait()


def pivots_of(pressure_diag, squared):
    rows = pressure_diag.shape[0]
    chunks = squared.shape[0]
    return pl.pallas_call(
        pivot_kernel,
        out_shape=jax.ShapeDtypeStruct((PIVOT_SPACE * rows * chunks, LANES), jnp.float32),
        in_specs=[in_smem, in_vmem],
        out_specs=in_hbm,
        scratch_shapes=[pltpu.VMEM((rows * chunks, LANES), jnp.float32), pltpu.SemaphoreType.DMA],
        compiler_params=pltpu.CompilerParams(vmem_limit_bytes=ALL_BYTES),
        cost_estimate=pl.CostEstimate(flops=10**7, bytes_accessed=10**7, transcendentals=0),
        name="pivots",
    )(pressure_diag, squared)


def project_kernel(
    x, waves, first, pivots_in, there_in, back_in, out,
    there, back, pivots, ready, folded, source, spectra, there_sems, back_sems, pivot_sem, out_sems
):
    blocks, _, rows, _ = x.shape
    count = blocks * LANES
    half = count // 2
    chunks = count // LANES
    per = TILE // LANES
    groups = waves.shape[0]
    pairs = [(j // (groups // 2) * groups + j % (groups // 2), groups // 2) for j in range(groups)]
    pairs = [(a, a + step) for a, step in pairs]

    load_pivots = pltpu.make_async_copy(pivots_in.at[pl.ds(0, rows * chunks)], pivots, pivot_sem)
    loads = {t: pltpu.make_async_copy(there_in.at[t], there.at[t], there_sems.at[t]) for pair in pairs for t in pair}
    returns = [pltpu.make_async_copy(back_in.at[t], back.at[t], back_sems.at[t]) for t in range(back.shape[0])]
    for copy in loads.values():
        copy.start()
    load_pivots.start()
    for copy in returns:
        copy.start()

    def fold(g, carry):
        at = pl.ds(pl.multiple_of(g * LANES, LANES), LANES)
        for field in range(2):
            here = slice(field * rows, (field + 1) * rows)
            a = x[g, field].astype(jnp.float32)
            b = x[g + blocks // 2, field].astype(jnp.float32)
            folded[0, here, at] = (a + b).astype(jnp.bfloat16)
            folded[1, here, at] = (a - b).astype(jnp.bfloat16)
        return carry

    lax.fori_loop(0, blocks // 2, fold, 0)

    inverse_step = 1.0 / step_size
    for j, (a, b) in enumerate(pairs):
        loads[a].wait()
        loads[b].wait()
        lhs = folded.at[j // (groups // 2)]
        cosine = jnp.dot(lhs[...], there[a], preferred_element_type=jnp.float32)
        sine = jnp.dot(lhs[...], there[b], preferred_element_type=jnp.float32)
        wave = waves[j : j + 1, :]
        for tile, value in (
            (a, (cosine[:rows] + wave * sine[rows:]) * inverse_step),
            (b, (sine[:rows] - wave * cosine[rows:]) * inverse_step),
        ):
            for k in range(per):
                source[pl.ds(tile * per + k, rows, stride=chunks), :] = value[:, k * LANES : (k + 1) * LANES]

    load_pivots.wait()
    unroll = 8

    def forward(i, before):
        for k in range(unroll):
            at = pl.ds(pl.multiple_of((i * unroll + k) * chunks, chunks), chunks)
            before = pivots[at, :] * (source[at, :] + before)
            source[at, :] = before
        return before

    def backward(i, after):
        for k in range(unroll):
            j = rows - 1 - (i * unroll + k)
            at = pl.ds(pl.multiple_of(j * chunks, chunks), chunks)
            after = pivots[at, :] * after - source[at, :]
            source[at, :] = after
        return after

    zero = jnp.zeros((chunks, LANES), jnp.float32)
    lax.fori_loop(0, rows // unroll, forward, zero)
    lax.fori_loop(0, rows // unroll, backward, zero)

    for j, (a, b) in enumerate(pairs):
        wave = waves[j : j + 1, :]
        for tile, other, sign in ((a, b, -1.0), (b, a, 1.0)):
            pressure = jnp.concatenate(
                [source[pl.ds(tile * per + k, rows, stride=chunks), :] for k in range(per)], 1
            )
            high = pressure.astype(jnp.bfloat16)
            low = (pressure - high.astype(jnp.float32)).astype(jnp.bfloat16)
            spectra[:rows, tile * TILE : (tile + 1) * TILE] = (
                jnp.dot(first[...], high, preferred_element_type=jnp.float32)
                + jnp.dot(first[...], low, preferred_element_type=jnp.float32)
            ).astype(jnp.bfloat16)
            spectra[rows:, other * TILE : (other + 1) * TILE] = (sign * wave * pressure).astype(jnp.bfloat16)

    def leave(g, field):
        return pltpu.make_async_copy(ready.at[g, field], out.at[g, field], out_sems.at[g, field])

    for tile in range(back.shape[0]):
        returns[tile].wait()
        even = jnp.dot(spectra[:, :half], back[tile, :half], preferred_element_type=jnp.float32)
        odd = jnp.dot(spectra[:, half:], back[tile, half:], preferred_element_type=jnp.float32)
        for k in range(per):
            at = slice(k * LANES, (k + 1) * LANES)
            g = tile * per + k
            for field in range(2):
                here = slice(field * rows, (field + 1) * rows)
                ready[g, field] = (even[here, at] + odd[here, at]).astype(jnp.bfloat16)
                leave(g, field).start()
                ready[g + blocks // 2, field] = (even[here, at] - odd[here, at]).astype(jnp.bfloat16)
                leave(g + blocks // 2, field).start()

    for g in range(blocks):
        for field in range(2):
            leave(g, field).wait()


def project(x, pivots, wall_first, there, back, waves):
    blocks, _, rows, lanes = x.shape
    count = blocks * lanes
    return pl.pallas_call(
        project_kernel,
        out_shape=jax.ShapeDtypeStruct(x.shape, jnp.bfloat16),
        in_specs=[in_vmem] * 3 + [in_hbm] * 3,
        out_specs=in_hbm,
        scratch_shapes=[
            pltpu.VMEM(there.shape, jnp.bfloat16),
            pltpu.VMEM(back.shape, jnp.bfloat16),
            pltpu.VMEM((rows * count // LANES, LANES), jnp.float32),
            pltpu.VMEM(x.shape, jnp.bfloat16),
            pltpu.VMEM((2, 2 * rows, count // 2), jnp.bfloat16),
            pltpu.VMEM((rows * count // LANES, LANES), jnp.float32),
            pltpu.VMEM((2 * rows, count), jnp.bfloat16),
            pltpu.SemaphoreType.DMA((there.shape[0],)),
            pltpu.SemaphoreType.DMA((back.shape[0],)),
            pltpu.SemaphoreType.DMA,
            pltpu.SemaphoreType.DMA((blocks, 2)),
        ],
        compiler_params=pltpu.CompilerParams(vmem_limit_bytes=MOST_BYTES),
        cost_estimate=pl.CostEstimate(
            flops=4 * rows * count * count, bytes_accessed=4 * there.size + 8 * x.size, transcendentals=0
        ),
        name="project",
    )(x, waves, wall_first, pivots, there, back)


def correct_kernel(result_in, star, change_in, result, change, ready, loads, sems):
    planes = star.shape[1]
    group = 4
    pieces = [(field, pl.ds(start, group)) for start in range(0, planes, group) for field in range(2)]
    arrive = [
        pltpu.make_async_copy(change_in.at[pl.ds(start, group)], change.at[pl.ds(start, group)], loads.at[start // group])
        for start in range(0, planes, group)
    ]
    depart = [
        pltpu.make_async_copy(ready.at[field, here], result.at[field + 1, here], sems.at[i])
        for i, (field, here) in enumerate(pieces)
    ]
    for copy in arrive:
        copy.start()
    for i, (field, here) in enumerate(pieces):
        if field == 0:
            arrive[i // 2].wait()
        ready[field, here] = (
            star[field, here].astype(jnp.float32) + change[here, field].astype(jnp.float32)
        ).astype(jnp.bfloat16)
        depart[i].start()
    for copy in depart:
        copy.wait()


def correct(result, star, change):
    planes = star.shape[1]
    return pl.pallas_call(
        correct_kernel,
        out_shape=jax.ShapeDtypeStruct(result.shape, jnp.bfloat16),
        in_specs=[in_hbm, in_vmem, in_hbm],
        out_specs=in_hbm,
        input_output_aliases={0: 0},
        scratch_shapes=[
            pltpu.VMEM(change.shape, jnp.bfloat16),
            pltpu.VMEM(star.shape, jnp.bfloat16),
            pltpu.SemaphoreType.DMA((planes // 4,)),
            pltpu.SemaphoreType.DMA((2 * planes // 4,)),
        ],
        compiler_params=pltpu.CompilerParams(vmem_limit_bytes=LAST_BYTES),
        name="correct",
    )(result, star, change)


def across(x):
    blocks, fields, rows, lanes = x.shape
    moved = lax.all_to_all(x.reshape(blocks, fields * rows, lanes), "gz", split_axis=0, concat_axis=0, tiled=True)
    return moved.reshape(x.shape)


def on_device(velocity, base_flow, wall_second, wall_first, rescale, pressure_diag):
    groups, slabs = lax.axis_size("grp"), lax.axis_size("gx")
    place = lax.axis_index("grp") * slabs + lax.axis_index("gx")
    ends = groups * slabs - 1
    flags = jnp.stack(
        [
            jnp.where(place == 0, 1, jnp.where(place == slabs, 2, 0)),
            jnp.where((place == slabs - 1) | (place == ends), 1, 0),
        ]
    ).astype(jnp.int32)
    up = [(i, i + 1) for i in range(ends)]
    down = [(i + 1, i) for i in range(ends)]
    lower = lax.ppermute(velocity[1:, -2:], ("grp", "gx"), up)
    upper = lax.ppermute(velocity[1:, :2], ("grp", "gx"), down)
    stream_lower = lax.ppermute(velocity[:1, -2:], ("grp", "gx"), up)
    stream_upper = lax.ppermute(velocity[:1, :2], ("grp", "gx"), down)
    flow = jnp.broadcast_to((base_flow * (step_size / 12.0))[:, None], (base_flow.shape[0], LANES))
    there, back, waves, squared = (jnp.asarray(t) for t in tables(lax.axis_size("gz") * velocity.shape[3]))

    star, send = advance_inner(velocity, flow, wall_second, wall_first)
    star, send = advance_outer(flags, velocity, lower, upper, flow, wall_second, wall_first, rescale, star, send)
    pencils = across(send)
    pivots = pivots_of(pressure_diag, squared)
    result = advance_stream(flags, velocity, stream_lower, stream_upper, flow, wall_second, rescale)
    change = across(project(pencils, pivots, wall_first, there, back, waves))
    return correct(result, star, change)


def solution(mesh):
    return jax.shard_map(
        on_device,
        mesh=mesh,
        in_specs=(P(None, ("grp", "gx"), None, "gz"), P(), P(), P(), P(), P()),
        out_specs=P(None, ("grp", "gx"), None, "gz"),
        check_vma=False,
    )
```

```python
import functools
import math

import jax
import jax.numpy as jnp
import ml_dtypes
import numpy as np
from jax import lax
from jax.experimental import pallas as pl
from jax.experimental.pallas import tpu as pltpu
from jax.sharding import PartitionSpec as P

step_size = 0.25
viscosity = 0.4
LANES = 128
TILE = 256
ALL_BYTES = 62914560
MOST_BYTES = 51000000
LAST_BYTES = 53000000
EDGE_BYTES = 54500000
PIVOT_SPACE = 6
SMALL_BYTES = 12 * 1024 * 1024


def mode_columns(count):
    quarter = count // 4
    even = 2 * np.arange(quarter)
    odd = even + 1
    sine_even = even.copy()
    sine_even[0] = count // 2
    is_sine = np.concatenate([np.zeros(quarter), np.ones(quarter), np.zeros(quarter), np.ones(quarter)]).astype(bool)
    is_sine[quarter] = False
    return np.concatenate([even, sine_even, odd, odd]).astype(np.int64), is_sine


@functools.lru_cache(maxsize=None)
def tables(count):
    half = count // 2
    mode, is_sine = mode_columns(count)
    z = np.arange(half, dtype=np.int64)
    angle = (z[:, None] * mode[None, :] % count).astype(np.float64) * (2.0 * math.pi / count)
    cosine, sine = np.cos(angle), np.sin(angle)
    own = np.where(is_sine[None, :], sine, cosine) / math.sqrt(count)
    signed = np.where((mode == 0) | (mode == half), 0, mode) * (2.0 * math.pi / count)
    weight = np.where((mode == 0) | (mode == half), 1.0, 2.0)
    cosines = np.concatenate([np.arange(count // 4), half + np.arange(count // 4)])
    waves = signed[cosines].reshape(-1, TILE)
    to_modes = [own[:, start : start + TILE] for start in range(0, count, TILE)]
    back = -step_size * own * weight
    from_modes = [
        np.concatenate([back[start : start + TILE, :half].T, back[start : start + TILE, half:].T], 0)
        for start in range(0, half, TILE)
    ]
    folded = np.minimum(mode, count - mode).astype(np.float64) * (2.0 * math.pi / count)
    return (
        np.stack(to_modes).astype(np.float32).astype(ml_dtypes.bfloat16),
        np.stack(from_modes).astype(np.float32).astype(ml_dtypes.bfloat16),
        waves.astype(np.float32),
        (folded * folded).astype(np.float32).reshape(count // LANES, LANES),
    )


def provisional(pad, at, field, flow, second, acc, store):
    rows = second.shape[0]
    strip = 80
    bend_scale = step_size * viscosity / 12.0
    normal_scale = step_size * viscosity
    both = jnp.concatenate([pad(field, at), pad(field, at + 1)], 1)
    acc[...] = jnp.dot(second[...], both, preferred_element_type=jnp.float32)
    for row in range(0, rows, strip):
        here = pl.ds(row, strip)
        ghost = [pad(field, at + k - 2, here).astype(jnp.float32) for k in range(6)]
        drift = flow[here, :]
        near_low = 16.0 * bend_scale + 8.0 * drift
        near_high = 16.0 * bend_scale - 8.0 * drift
        for half in range(2):
            far_low, low, centre, high, far_high = ghost[half : half + 5]
            new = (
                (1.0 - 30.0 * bend_scale) * centre
                + normal_scale * acc[here, half * LANES : (half + 1) * LANES]
                + near_low * low
                + near_high * high
                + (drift - bend_scale) * far_high
                - (drift + bend_scale) * far_low
            )
            store(field, at + half, here, new.astype(jnp.bfloat16))


def slope_pair(first, star, send, at):
    both = jnp.concatenate([star[0, at], star[0, at + 1]], 1)
    out = jnp.dot(first[...], both, preferred_element_type=jnp.float32).astype(jnp.bfloat16)
    send[at, 0] = out[:, :LANES]
    send[at + 1, 0] = out[:, LANES:]


def inner_kernel(
    velocity, flow_in, second_in, first_in, star_out, send_out, vel, star, send, acc, flow, second, first, loads, fixed_sems, sems
):
    planes = vel.shape[1]
    fixed = [
        pltpu.make_async_copy(source, target, fixed_sems.at[i])
        for i, (source, target) in enumerate(((second_in, second), (flow_in, flow), (first_in, first)))
    ]
    for copy in fixed:
        copy.start()

    def load(i):
        here = pl.ds(2 * i, 2)
        return pltpu.make_async_copy(velocity.at[pl.ds(1, 2), here], vel.at[:, here], loads.at[i])

    for i in range(planes // 2):
        load(i).start()

    def pad(field, plane, here=slice(None)):
        return vel[field, plane, here, :]

    def store(field, plane, here, value):
        star[field, plane, here, :] = value
        if field == 1:
            send[plane, 1, here, :] = value

    def copies(i):
        here = pl.ds(2 * i, 2)
        return (
            pltpu.make_async_copy(send.at[here], send_out.at[here], sems.at[0, i]),
            pltpu.make_async_copy(star.at[:, here], star_out.at[:, here], sems.at[1, i]),
        )

    def pair(i, carry):
        load(i + 1).wait()
        for field in range(2):
            provisional(pad, 2 * i, field, flow, second, acc, store)
        slope_pair(first, star, send, 2 * i)
        for copy in copies(i):
            copy.start()
        return carry

    def settle(i, carry):
        for copy in copies(i):
            copy.wait()
        return carry

    for copy in fixed:
        copy.wait()
    load(0).wait()
    load(1).wait()
    lax.fori_loop(1, planes // 2 - 1, pair, 0)
    lax.fori_loop(1, planes // 2 - 1, settle, 0)


def rim_loads(velocity, fields, planes, lower, upper, rim, sems):
    return [
        pltpu.make_async_copy(velocity.at[fields, pl.ds(0, 4)], rim.at[:, 0, pl.ds(2, 4)], sems.at[0]),
        pltpu.make_async_copy(velocity.at[fields, pl.ds(planes - 4, 4)], rim.at[:, 1, pl.ds(0, 4)], sems.at[1]),
        pltpu.make_async_copy(lower, rim.at[:, 0, pl.ds(0, 2)], sems.at[2]),
        pltpu.make_async_copy(upper, rim.at[:, 1, pl.ds(4, 2)], sems.at[3]),
    ]


def fix_rims(flags, rescale, rim):
    fields = rim.shape[0]

    @pl.when(flags[0] == 1)
    def _():
        for field in range(fields):
            rim[field, 0, 0] = rim[field, 0, 2]
            rim[field, 0, 1] = rim[field, 0, 2]

    @pl.when(flags[0] == 2)
    def _():
        for field in range(fields):
            both = jnp.concatenate([rim[field, 0, 0], rim[field, 0, 1]], 1)
            inflow = jnp.dot(rescale[...], both, preferred_element_type=jnp.float32).astype(jnp.bfloat16)
            rim[field, 0, 0] = inflow[:, :LANES]
            rim[field, 0, 1] = inflow[:, LANES:]

    @pl.when(flags[1] == 1)
    def _():
        for field in range(fields):
            rim[field, 1, 4] = rim[field, 1, 3]
            rim[field, 1, 5] = rim[field, 1, 3]


def outer_kernel(
    flags, velocity, lower, upper, flow, second, first, rescale, star_in, send_in, star, send, rim, edge, away, acc, loads, sems
):
    planes = velocity.shape[1]
    arrive = rim_loads(velocity, pl.ds(1, 2), planes, lower, upper, rim, loads)
    for copy in arrive:
        copy.start()
    for copy in arrive:
        copy.wait()
    fix_rims(flags, rescale, rim)
    copies = []
    for side in range(2):
        base = 2 * side

        def pad(field, plane, here=slice(None)):
            return rim[field, side, plane - base + 2, here, :]

        def store(field, plane, here, value):
            edge[field, plane, here, :] = value
            if field == 1:
                away[plane, 1, here, :] = value

        for field in range(2):
            provisional(pad, base, field, flow, second, acc, store)
        slope_pair(first, edge, away, base)
        here, there = pl.ds(base, 2), pl.ds(0 if side == 0 else planes - 2, 2)
        for source, target in ((away.at[here], send.at[there]), (edge.at[:, here], star.at[:, there])):
            copies.append(pltpu.make_async_copy(source, target, sems.at[len(copies)]))
            copies[-1].start()
    for copy in copies:
        copy.wait()


def stream_kernel(flags, velocity, lower, upper, flow, second, rescale, result, vel, rim, star, acc, loads, sems):
    planes = velocity.shape[1]
    arrive = rim_loads(velocity, pl.ds(0, 1), planes, lower, upper, rim, loads)
    arrive.append(pltpu.make_async_copy(velocity.at[0], vel, loads.at[4]))
    for copy in arrive:
        copy.start()
    for copy in arrive:
        copy.wait()
    fix_rims(flags, rescale, rim)

    def store(field, plane, here, value):
        star[plane, here, :] = value

    def pad(field, plane, here=slice(None)):
        return vel[plane, here, :]

    def copy(i):
        here = pl.ds(2 * i, 2)
        return pltpu.make_async_copy(star.at[here], result.at[0, here], sems.at[i])

    def pair(i, carry):
        provisional(pad, 2 * i, 0, flow, second, acc, store)
        copy(i).start()
        return carry

    def settle(i, carry):
        copy(i).wait()
        return carry

    lax.fori_loop(1, planes // 2 - 1, pair, 0)
    for side in range(2):
        base = 0 if side == 0 else planes - 2

        def rim_pad(field, plane, here=slice(None)):
            return rim[field, side, plane - base + 2, here, :]

        provisional(rim_pad, base, 0, flow, second, acc, store)
        copy(base // 2).start()
    lax.fori_loop(0, planes // 2, settle, 0)


in_vmem = pl.BlockSpec(memory_space=pltpu.VMEM)
in_smem = pl.BlockSpec(memory_space=pltpu.SMEM)
in_hbm = pl.BlockSpec(memory_space=pltpu.HBM)


def cost_of(fields, planes, rows, lanes):
    return pl.CostEstimate(
        flops=fields * planes * rows * lanes * 2 * rows, bytes_accessed=4 * fields * planes * rows * lanes, transcendentals=0
    )


def advance_inner(velocity, flow, second, first):
    _, planes, rows, lanes = velocity.shape
    return pl.pallas_call(
        inner_kernel,
        out_shape=[
            jax.ShapeDtypeStruct((2, planes, rows, lanes), jnp.bfloat16),
            jax.ShapeDtypeStruct((planes, 2, rows, lanes), jnp.bfloat16),
        ],
        in_specs=[in_hbm] * 4,
        out_specs=[in_hbm] * 2,
        scratch_shapes=[
            pltpu.VMEM((2, planes, rows, lanes), jnp.bfloat16),
            pltpu.VMEM((2, planes, rows, lanes), jnp.bfloat16),
            pltpu.VMEM((planes, 2, rows, lanes), jnp.bfloat16),
            pltpu.VMEM((rows, 2 * lanes), jnp.float32),
            pltpu.VMEM(flow.shape, jnp.float32),
            pltpu.VMEM(second.shape, jnp.bfloat16),
            pltpu.VMEM(first.shape, jnp.bfloat16),
            pltpu.SemaphoreType.DMA((planes // 2,)),
            pltpu.SemaphoreType.DMA((3,)),
            pltpu.SemaphoreType.DMA((2, planes // 2)),
        ],
        compiler_params=pltpu.CompilerParams(vmem_limit_bytes=ALL_BYTES),
        cost_estimate=cost_of(2, planes, rows, lanes),
        name="advance_inner",
    )(velocity, flow, second, first)


def advance_outer(flags, velocity, lower, upper, flow, second, first, rescale, star, send):
    _, planes, rows, lanes = velocity.shape
    return pl.pallas_call(
        outer_kernel,
        out_shape=[
            jax.ShapeDtypeStruct(star.shape, jnp.bfloat16),
            jax.ShapeDtypeStruct(send.shape, jnp.bfloat16),
        ],
        in_specs=[in_smem] + [in_hbm] * 3 + [in_vmem] * 4 + [in_hbm] * 2,
        out_specs=[in_hbm] * 2,
        input_output_aliases={8: 0, 9: 1},
        scratch_shapes=[
            pltpu.VMEM((2, 2, 6, rows, lanes), jnp.bfloat16),
            pltpu.VMEM((2, 4, rows, lanes), jnp.bfloat16),
            pltpu.VMEM((4, 2, rows, lanes), jnp.bfloat16),
            pltpu.VMEM((rows, 2 * lanes), jnp.float32),
            pltpu.SemaphoreType.DMA((4,)),
            pltpu.SemaphoreType.DMA((4,)),
        ],
        compiler_params=pltpu.CompilerParams(vmem_limit_bytes=EDGE_BYTES),
        cost_estimate=cost_of(2, 4, rows, lanes),
        name="advance_outer",
    )(flags, velocity, lower, upper, flow, second, first, rescale, star, send)


def advance_stream(flags, velocity, lower, upper, flow, second, rescale):
    _, planes, rows, lanes = velocity.shape
    return pl.pallas_call(
        stream_kernel,
        out_shape=jax.ShapeDtypeStruct(velocity.shape, jnp.bfloat16),
        in_specs=[in_smem] + [in_hbm] * 3 + [in_vmem] * 3,
        out_specs=in_hbm,
        scratch_shapes=[
            pltpu.VMEM((planes, rows, lanes), jnp.bfloat16),
            pltpu.VMEM((1, 2, 6, rows, lanes), jnp.bfloat16),
            pltpu.VMEM((planes, rows, lanes), jnp.bfloat16),
            pltpu.VMEM((rows, 2 * lanes), jnp.float32),
            pltpu.SemaphoreType.DMA((5,)),
            pltpu.SemaphoreType.DMA((planes // 2,)),
        ],
        compiler_params=pltpu.CompilerParams(vmem_limit_bytes=EDGE_BYTES),
        cost_estimate=cost_of(1, planes, rows, lanes),
        name="advance_stream",
    )(flags, velocity, lower, upper, flow, second, rescale)


def pivot_kernel(diag, squared, out, pivots, sem):
    rows = diag.shape[0]
    chunks = squared.shape[0]

    def step(j, before):
        now = 1.0 / ((2.0 + diag[j]) + squared[...] - before)
        pivots[pl.ds(pl.multiple_of(j * chunks, chunks), chunks), :] = now
        return now

    lax.fori_loop(0, rows, step, jnp.zeros_like(squared[...]))
    copy = pltpu.make_async_copy(pivots, out.at[pl.ds(0, rows * chunks)], sem)
    copy.start()
    copy.wait()


def pivots_of(pressure_diag, squared):
    rows = pressure_diag.shape[0]
    chunks = squared.shape[0]
    return pl.pallas_call(
        pivot_kernel,
        out_shape=jax.ShapeDtypeStruct((PIVOT_SPACE * rows * chunks, LANES), jnp.float32),
        in_specs=[in_smem, in_vmem],
        out_specs=in_hbm,
        scratch_shapes=[pltpu.VMEM((rows * chunks, LANES), jnp.float32), pltpu.SemaphoreType.DMA],
        compiler_params=pltpu.CompilerParams(vmem_limit_bytes=ALL_BYTES),
        cost_estimate=pl.CostEstimate(flops=10**7, bytes_accessed=10**7, transcendentals=0),
        name="pivots",
    )(pressure_diag, squared)


def project_kernel(
    x, waves, first, pivots_in, there_in, back_in, result, out,
    there, back, pivots, folded, source, spectra, there_sems, back_sems, pivot_sem
):
    blocks, _, rows, _ = x.shape
    count = blocks * LANES
    half = count // 2
    chunks = count // LANES
    per = TILE // LANES
    groups = waves.shape[0]
    pairs = [(j // (groups // 2) * groups + j % (groups // 2), groups // 2) for j in range(groups)]
    pairs = [(a, a + step) for a, step in pairs]

    load_pivots = pltpu.make_async_copy(pivots_in.at[pl.ds(0, rows * chunks)], pivots, pivot_sem)
    loads = {t: pltpu.make_async_copy(there_in.at[t], there.at[t], there_sems.at[t]) for pair in pairs for t in pair}
    returns = [pltpu.make_async_copy(back_in.at[t], back.at[t], back_sems.at[t]) for t in range(back.shape[0])]
    for copy in loads.values():
        copy.start()
    load_pivots.start()
    for copy in returns:
        copy.start()

    def fold(g, carry):
        at = pl.ds(pl.multiple_of(g * LANES, LANES), LANES)
        for field in range(2):
            here = slice(field * rows, (field + 1) * rows)
            a = x[g, field].astype(jnp.float32)
            b = x[g + blocks // 2, field].astype(jnp.float32)
            folded[0, here, at] = (a + b).astype(jnp.bfloat16)
            folded[1, here, at] = (a - b).astype(jnp.bfloat16)
        return carry

    lax.fori_loop(0, blocks // 2, fold, 0)

    inverse_step = 1.0 / step_size
    for j, (a, b) in enumerate(pairs):
        loads[a].wait()
        loads[b].wait()
        lhs = folded.at[j // (groups // 2)]
        cosine = jnp.dot(lhs[...], there[a], preferred_element_type=jnp.float32)
        sine = jnp.dot(lhs[...], there[b], preferred_element_type=jnp.float32)
        wave = waves[j : j + 1, :]
        for tile, value in (
            (a, (cosine[:rows] + wave * sine[rows:]) * inverse_step),
            (b, (sine[:rows] - wave * cosine[rows:]) * inverse_step),
        ):
            for k in range(per):
                source[pl.ds(tile * per + k, rows, stride=chunks), :] = value[:, k * LANES : (k + 1) * LANES]

    load_pivots.wait()
    unroll = 8

    def forward(i, before):
        for k in range(unroll):
            at = pl.ds(pl.multiple_of((i * unroll + k) * chunks, chunks), chunks)
            before = pivots[at, :] * (source[at, :] + before)
            source[at, :] = before
        return before

    def backward(i, after):
        for k in range(unroll):
            j = rows - 1 - (i * unroll + k)
            at = pl.ds(pl.multiple_of(j * chunks, chunks), chunks)
            after = pivots[at, :] * after - source[at, :]
            source[at, :] = after
        return after

    zero = jnp.zeros((chunks, LANES), jnp.float32)
    lax.fori_loop(0, rows // unroll, forward, zero)
    lax.fori_loop(0, rows // unroll, backward, zero)

    twice = jnp.concatenate([first[...], first[...]], 1)
    for j, (a, b) in enumerate(pairs):
        wave = waves[j : j + 1, :]
        for tile, other, sign in ((a, b, -1.0), (b, a, 1.0)):
            pressure = jnp.concatenate(
                [source[pl.ds(tile * per + k, rows, stride=chunks), :] for k in range(per)], 1
            )
            high = pressure.astype(jnp.bfloat16)
            low = (pressure - high.astype(jnp.float32)).astype(jnp.bfloat16)
            both = jnp.concatenate([high, low], 0)
            spectra[:rows, tile * TILE : (tile + 1) * TILE] = jnp.dot(
                twice, both, preferred_element_type=jnp.float32
            ).astype(jnp.bfloat16)
            spectra[rows:, other * TILE : (other + 1) * TILE] = (sign * wave * pressure).astype(jnp.bfloat16)

    for tile in range(back.shape[0]):
        returns[tile].wait()
        even = jnp.dot(spectra[:, :half], back[tile, :half], preferred_element_type=jnp.float32)
        odd = jnp.dot(spectra[:, half:], back[tile, half:], preferred_element_type=jnp.float32)
        for k in range(per):
            at = slice(k * LANES, (k + 1) * LANES)
            g = tile * per + k
            for field in range(2):
                here = slice(field * rows, (field + 1) * rows)
                out[g, field] = (even[here, at] + odd[here, at]).astype(jnp.bfloat16)
                out[g + blocks // 2, field] = (even[here, at] - odd[here, at]).astype(jnp.bfloat16)


def project(x, pivots, wall_first, there, back, waves, result):
    blocks, _, rows, lanes = x.shape
    count = blocks * lanes
    return pl.pallas_call(
        project_kernel,
        out_shape=jax.ShapeDtypeStruct(x.shape, jnp.bfloat16),
        in_specs=[in_vmem] * 3 + [in_hbm] * 4,
        out_specs=in_vmem,
        scratch_shapes=[
            pltpu.VMEM(there.shape, jnp.bfloat16),
            pltpu.VMEM(back.shape, jnp.bfloat16),
            pltpu.VMEM((rows * count // LANES, LANES), jnp.float32),
            pltpu.VMEM((2, 2 * rows, count // 2), jnp.bfloat16),
            pltpu.VMEM((rows * count // LANES, LANES), jnp.float32),
            pltpu.VMEM((2 * rows, count), jnp.bfloat16),
            pltpu.SemaphoreType.DMA((there.shape[0],)),
            pltpu.SemaphoreType.DMA((back.shape[0],)),
            pltpu.SemaphoreType.DMA,
        ],
        compiler_params=pltpu.CompilerParams(vmem_limit_bytes=MOST_BYTES),
        cost_estimate=pl.CostEstimate(
            flops=4 * rows * count * count, bytes_accessed=4 * there.size + 8 * x.size, transcendentals=0
        ),
        name="project",
    )(x, waves, wall_first, pivots, there, back, result)


def correct_kernel(result_in, star, change_in, result, change, ready, loads, sems):
    planes = star.shape[1]
    group = 4
    pieces = [(field, pl.ds(start, group)) for start in range(0, planes, group) for field in range(2)]
    arrive = [
        pltpu.make_async_copy(change_in.at[pl.ds(start, group)], change.at[pl.ds(start, group)], loads.at[start // group])
        for start in range(0, planes, group)
    ]
    depart = [
        pltpu.make_async_copy(ready.at[field, here], result.at[field + 1, here], sems.at[i])
        for i, (field, here) in enumerate(pieces)
    ]
    for copy in arrive:
        copy.start()
    for i, (field, here) in enumerate(pieces):
        if field == 0:
            arrive[i // 2].wait()
        ready[field, here] = (
            star[field, here].astype(jnp.float32) + change[here, field].astype(jnp.float32)
        ).astype(jnp.bfloat16)
        depart[i].start()
    for copy in depart:
        copy.wait()


def correct(result, star, change):
    planes = star.shape[1]
    return pl.pallas_call(
        correct_kernel,
        out_shape=jax.ShapeDtypeStruct(result.shape, jnp.bfloat16),
        in_specs=[in_hbm, in_vmem, in_hbm],
        out_specs=in_hbm,
        input_output_aliases={0: 0},
        scratch_shapes=[
            pltpu.VMEM(change.shape, jnp.bfloat16),
            pltpu.VMEM(star.shape, jnp.bfloat16),
            pltpu.SemaphoreType.DMA((planes // 4,)),
            pltpu.SemaphoreType.DMA((2 * planes // 4,)),
        ],
        compiler_params=pltpu.CompilerParams(vmem_limit_bytes=LAST_BYTES),
        name="correct",
    )(result, star, change)


def across(x):
    blocks, fields, rows, lanes = x.shape
    moved = lax.all_to_all(x.reshape(blocks, fields * rows, lanes), "gz", split_axis=0, concat_axis=0, tiled=True)
    return moved.reshape(x.shape)


def on_device(velocity, base_flow, wall_second, wall_first, rescale, pressure_diag):
    groups, slabs = lax.axis_size("grp"), lax.axis_size("gx")
    place = lax.axis_index("grp") * slabs + lax.axis_index("gx")
    ends = groups * slabs - 1
    flags = jnp.stack(
        [
            jnp.where(place == 0, 1, jnp.where(place == slabs, 2, 0)),
            jnp.where((place == slabs - 1) | (place == ends), 1, 0),
        ]
    ).astype(jnp.int32)
    up = [(i, i + 1) for i in range(ends)]
    down = [(i + 1, i) for i in range(ends)]
    lower = lax.ppermute(velocity[1:, -2:], ("grp", "gx"), up)
    upper = lax.ppermute(velocity[1:, :2], ("grp", "gx"), down)
    stream_lower = lax.ppermute(velocity[:1, -2:], ("grp", "gx"), up)
    stream_upper = lax.ppermute(velocity[:1, :2], ("grp", "gx"), down)
    flow = jnp.broadcast_to((base_flow * (step_size / 12.0))[:, None], (base_flow.shape[0], LANES))
    there, back, waves, squared = (jnp.asarray(t) for t in tables(lax.axis_size("gz") * velocity.shape[3]))

    star, send = advance_inner(velocity, flow, wall_second, wall_first)
    star, send = advance_outer(flags, velocity, lower, upper, flow, wall_second, wall_first, rescale, star, send)
    pencils = across(send)
    pivots = pivots_of(pressure_diag, squared)
    result = advance_stream(flags, velocity, stream_lower, stream_upper, flow, wall_second, rescale)
    change = across(project(pencils, pivots, wall_first, there, back, waves, result))
    return correct(result, star, change)


def solution(mesh):
    return jax.shard_map(
        on_device,
        mesh=mesh,
        in_specs=(P(None, ("grp", "gx"), None, "gz"), P(), P(), P(), P(), P()),
        out_specs=P(None, ("grp", "gx"), None, "gz"),
        check_vma=False,
    )
```

```python
import functools
import math

import jax
import jax.numpy as jnp
import ml_dtypes
import numpy as np
from jax import lax
from jax.experimental import pallas as pl
from jax.experimental.pallas import tpu as pltpu
from jax.sharding import PartitionSpec as P

step_size = 0.25
viscosity = 0.4
LANES = 128
TILE = 256
ALL_BYTES = 62914560
MOST_BYTES = 51000000
LAST_BYTES = 53000000
EDGE_BYTES = 54500000
PIVOT_SPACE = 6
SMALL_BYTES = 12 * 1024 * 1024


def mode_columns(count):
    quarter = count // 4
    even = 2 * np.arange(quarter)
    odd = even + 1
    sine_even = even.copy()
    sine_even[0] = count // 2
    is_sine = np.concatenate([np.zeros(quarter), np.ones(quarter), np.zeros(quarter), np.ones(quarter)]).astype(bool)
    is_sine[quarter] = False
    return np.concatenate([even, sine_even, odd, odd]).astype(np.int64), is_sine


@functools.lru_cache(maxsize=None)
def tables(count):
    half = count // 2
    mode, is_sine = mode_columns(count)
    z = np.arange(half, dtype=np.int64)
    angle = (z[:, None] * mode[None, :] % count).astype(np.float64) * (2.0 * math.pi / count)
    cosine, sine = np.cos(angle), np.sin(angle)
    own = np.where(is_sine[None, :], sine, cosine) / math.sqrt(count)
    signed = np.where((mode == 0) | (mode == half), 0, mode) * (2.0 * math.pi / count)
    weight = np.where((mode == 0) | (mode == half), 1.0, 2.0)
    cosines = np.concatenate([np.arange(count // 4), half + np.arange(count // 4)])
    waves = signed[cosines].reshape(-1, TILE)
    to_modes = [own[:, start : start + TILE] for start in range(0, count, TILE)]
    back = -step_size * own * weight
    from_modes = [
        np.concatenate([back[start : start + TILE, :half].T, back[start : start + TILE, half:].T], 0)
        for start in range(0, half, TILE)
    ]
    folded = np.minimum(mode, count - mode).astype(np.float64) * (2.0 * math.pi / count)
    return (
        np.stack(to_modes).astype(np.float32).astype(ml_dtypes.bfloat16),
        np.stack(from_modes).astype(np.float32).astype(ml_dtypes.bfloat16),
        waves.astype(np.float32),
        (folded * folded).astype(np.float32).reshape(count // LANES, LANES),
    )


def provisional(pad, at, field, flow, second, acc, store):
    rows = second.shape[0]
    strip = 80
    bend_scale = step_size * viscosity / 12.0
    normal_scale = step_size * viscosity
    both = jnp.concatenate([pad(field, at), pad(field, at + 1)], 1)
    acc[...] = jnp.dot(second[...], both, preferred_element_type=jnp.float32)
    for row in range(0, rows, strip):
        here = pl.ds(row, strip)
        ghost = [pad(field, at + k - 2, here).astype(jnp.float32) for k in range(6)]
        drift = (step_size / 12.0) * flow[here, :]
        near_low = 16.0 * bend_scale + 8.0 * drift
        near_high = 16.0 * bend_scale - 8.0 * drift
        for half in range(2):
            far_low, low, centre, high, far_high = ghost[half : half + 5]
            new = (
                (1.0 - 30.0 * bend_scale) * centre
                + normal_scale * acc[here, half * LANES : (half + 1) * LANES]
                + near_low * low
                + near_high * high
                + (drift - bend_scale) * far_high
                - (drift + bend_scale) * far_low
            )
            store(field, at + half, here, new.astype(jnp.bfloat16))


def slope_pair(first, star, send, at):
    both = jnp.concatenate([star[0, at], star[0, at + 1]], 1)
    out = jnp.dot(first[...], both, preferred_element_type=jnp.float32).astype(jnp.bfloat16)
    send[at, 0] = out[:, :LANES]
    send[at + 1, 0] = out[:, LANES:]


def inner_kernel(
    velocity, flow_in, second_in, first_in, star_out, send_out, vel, star, send, acc, flow, second, first, loads, fixed_sems, sems
):
    planes = vel.shape[1]
    fixed = [
        pltpu.make_async_copy(source, target, fixed_sems.at[i])
        for i, (source, target) in enumerate(((second_in, second), (flow_in, flow), (first_in, first)))
    ]
    for copy in fixed:
        copy.start()

    def load(i):
        here = pl.ds(2 * i, 2)
        return pltpu.make_async_copy(velocity.at[pl.ds(1, 2), here], vel.at[:, here], loads.at[i])

    for i in range(planes // 2):
        load(i).start()

    def pad(field, plane, here=slice(None)):
        return vel[field, plane, here, :]

    def store(field, plane, here, value):
        star[field, plane, here, :] = value
        if field == 1:
            send[plane, 1, here, :] = value

    def copies(i):
        here = pl.ds(2 * i, 2)
        return (
            pltpu.make_async_copy(send.at[here], send_out.at[here], sems.at[0, i]),
            pltpu.make_async_copy(star.at[:, here], star_out.at[:, here], sems.at[1, i]),
        )

    def pair(i, carry):
        load(i + 1).wait()
        for field in range(2):
            provisional(pad, 2 * i, field, flow, second, acc, store)
        slope_pair(first, star, send, 2 * i)
        for copy in copies(i):
            copy.start()
        return carry

    def settle(i, carry):
        for copy in copies(i):
            copy.wait()
        return carry

    for copy in fixed:
        copy.wait()
    load(0).wait()
    load(1).wait()
    lax.fori_loop(1, planes // 2 - 1, pair, 0)
    lax.fori_loop(1, planes // 2 - 1, settle, 0)


def rim_loads(velocity, fields, planes, lower, upper, rim, sems):
    return [
        pltpu.make_async_copy(velocity.at[fields, pl.ds(0, 4)], rim.at[:, 0, pl.ds(2, 4)], sems.at[0]),
        pltpu.make_async_copy(velocity.at[fields, pl.ds(planes - 4, 4)], rim.at[:, 1, pl.ds(0, 4)], sems.at[1]),
        pltpu.make_async_copy(lower, rim.at[:, 0, pl.ds(0, 2)], sems.at[2]),
        pltpu.make_async_copy(upper, rim.at[:, 1, pl.ds(4, 2)], sems.at[3]),
    ]


def fix_rims(flags, rescale, rim):
    fields = rim.shape[0]

    @pl.when(flags[0] == 1)
    def _():
        for field in range(fields):
            rim[field, 0, 0] = rim[field, 0, 2]
            rim[field, 0, 1] = rim[field, 0, 2]

    @pl.when(flags[0] == 2)
    def _():
        for field in range(fields):
            both = jnp.concatenate([rim[field, 0, 0], rim[field, 0, 1]], 1)
            inflow = jnp.dot(rescale[...], both, preferred_element_type=jnp.float32).astype(jnp.bfloat16)
            rim[field, 0, 0] = inflow[:, :LANES]
            rim[field, 0, 1] = inflow[:, LANES:]

    @pl.when(flags[1] == 1)
    def _():
        for field in range(fields):
            rim[field, 1, 4] = rim[field, 1, 3]
            rim[field, 1, 5] = rim[field, 1, 3]


def outer_kernel(
    flags, velocity, lower, upper, flow, second, first, rescale, star_in, send_in, star, send, rim, edge, away, acc, loads, sems
):
    planes = velocity.shape[1]
    arrive = rim_loads(velocity, pl.ds(1, 2), planes, lower, upper, rim, loads)
    for copy in arrive:
        copy.start()
    for copy in arrive:
        copy.wait()
    fix_rims(flags, rescale, rim)
    copies = []
    for side in range(2):
        base = 2 * side

        def pad(field, plane, here=slice(None)):
            return rim[field, side, plane - base + 2, here, :]

        def store(field, plane, here, value):
            edge[field, plane, here, :] = value
            if field == 1:
                away[plane, 1, here, :] = value

        for field in range(2):
            provisional(pad, base, field, flow, second, acc, store)
        slope_pair(first, edge, away, base)
        here, there = pl.ds(base, 2), pl.ds(0 if side == 0 else planes - 2, 2)
        for source, target in ((away.at[here], send.at[there]), (edge.at[:, here], star.at[:, there])):
            copies.append(pltpu.make_async_copy(source, target, sems.at[len(copies)]))
            copies[-1].start()
    for copy in copies:
        copy.wait()


def stream_inner_kernel(velocity, flow, second, result, vel, star, acc, load, sems):
    planes = velocity.shape[1]
    arrive = pltpu.make_async_copy(velocity.at[0], vel, load)
    arrive.start()
    arrive.wait()

    def store(field, plane, here, value):
        star[plane, here, :] = value

    def pad(field, plane, here=slice(None)):
        return vel[plane, here, :]

    def copy(i):
        here = pl.ds(2 * i, 2)
        return pltpu.make_async_copy(star.at[here], result.at[0, here], sems.at[i])

    def pair(i, carry):
        provisional(pad, 2 * i, 0, flow, second, acc, store)
        copy(i).start()
        return carry

    def settle(i, carry):
        copy(i).wait()
        return carry

    lax.fori_loop(1, planes // 2 - 1, pair, 0)
    lax.fori_loop(1, planes // 2 - 1, settle, 0)


def stream_outer_kernel(flags, velocity, lower, upper, flow, second, rescale, result_in, result, rim, star, acc, loads, sems):
    planes = velocity.shape[1]
    arrive = rim_loads(velocity, pl.ds(0, 1), planes, lower, upper, rim, loads)
    for copy in arrive:
        copy.start()
    for copy in arrive:
        copy.wait()
    fix_rims(flags, rescale, rim)
    copies = []
    for side in range(2):
        base = 2 * side

        def store(field, plane, here, value):
            star[plane, here, :] = value

        def pad(field, plane, here=slice(None)):
            return rim[field, side, plane - base + 2, here, :]

        provisional(pad, base, 0, flow, second, acc, store)
        here, there = pl.ds(base, 2), pl.ds(0 if side == 0 else planes - 2, 2)
        copies.append(pltpu.make_async_copy(star.at[here], result.at[0, there], sems.at[side]))
        copies[-1].start()
    for copy in copies:
        copy.wait()


in_vmem = pl.BlockSpec(memory_space=pltpu.VMEM)
in_smem = pl.BlockSpec(memory_space=pltpu.SMEM)
in_hbm = pl.BlockSpec(memory_space=pltpu.HBM)


def cost_of(fields, planes, rows, lanes):
    return pl.CostEstimate(
        flops=fields * planes * rows * lanes * 2 * rows, bytes_accessed=4 * fields * planes * rows * lanes, transcendentals=0
    )


def advance_inner(velocity, flow, second, first):
    _, planes, rows, lanes = velocity.shape
    return pl.pallas_call(
        inner_kernel,
        out_shape=[
            jax.ShapeDtypeStruct((2, planes, rows, lanes), jnp.bfloat16),
            jax.ShapeDtypeStruct((planes, 2, rows, lanes), jnp.bfloat16),
        ],
        in_specs=[in_hbm] * 4,
        out_specs=[in_hbm] * 2,
        scratch_shapes=[
            pltpu.VMEM((2, planes, rows, lanes), jnp.bfloat16),
            pltpu.VMEM((2, planes, rows, lanes), jnp.bfloat16),
            pltpu.VMEM((planes, 2, rows, lanes), jnp.bfloat16),
            pltpu.VMEM((rows, 2 * lanes), jnp.float32),
            pltpu.VMEM(flow.shape, jnp.float32),
            pltpu.VMEM(second.shape, jnp.bfloat16),
            pltpu.VMEM(first.shape, jnp.bfloat16),
            pltpu.SemaphoreType.DMA((planes // 2,)),
            pltpu.SemaphoreType.DMA((3,)),
            pltpu.SemaphoreType.DMA((2, planes // 2)),
        ],
        compiler_params=pltpu.CompilerParams(vmem_limit_bytes=ALL_BYTES),
        cost_estimate=cost_of(2, planes, rows, lanes),
        name="advance_inner",
    )(velocity, flow, second, first)


def advance_outer(flags, velocity, lower, upper, flow, second, first, rescale, star, send):
    _, planes, rows, lanes = velocity.shape
    return pl.pallas_call(
        outer_kernel,
        out_shape=[
            jax.ShapeDtypeStruct(star.shape, jnp.bfloat16),
            jax.ShapeDtypeStruct(send.shape, jnp.bfloat16),
        ],
        in_specs=[in_smem] + [in_hbm] * 3 + [in_vmem] * 4 + [in_hbm] * 2,
        out_specs=[in_hbm] * 2,
        input_output_aliases={8: 0, 9: 1},
        scratch_shapes=[
            pltpu.VMEM((2, 2, 6, rows, lanes), jnp.bfloat16),
            pltpu.VMEM((2, 4, rows, lanes), jnp.bfloat16),
            pltpu.VMEM((4, 2, rows, lanes), jnp.bfloat16),
            pltpu.VMEM((rows, 2 * lanes), jnp.float32),
            pltpu.SemaphoreType.DMA((4,)),
            pltpu.SemaphoreType.DMA((4,)),
        ],
        compiler_params=pltpu.CompilerParams(vmem_limit_bytes=EDGE_BYTES),
        cost_estimate=cost_of(2, 4, rows, lanes),
        name="advance_outer",
    )(flags, velocity, lower, upper, flow, second, first, rescale, star, send)


def advance_stream_inner(velocity, flow, second):
    _, planes, rows, lanes = velocity.shape
    return pl.pallas_call(
        stream_inner_kernel,
        out_shape=jax.ShapeDtypeStruct(velocity.shape, jnp.bfloat16),
        in_specs=[in_hbm] + [in_vmem] * 2,
        out_specs=in_hbm,
        scratch_shapes=[
            pltpu.VMEM((planes, rows, lanes), jnp.bfloat16),
            pltpu.VMEM((planes, rows, lanes), jnp.bfloat16),
            pltpu.VMEM((rows, 2 * lanes), jnp.float32),
            pltpu.SemaphoreType.DMA,
            pltpu.SemaphoreType.DMA((planes // 2,)),
        ],
        compiler_params=pltpu.CompilerParams(vmem_limit_bytes=EDGE_BYTES),
        cost_estimate=cost_of(1, planes, rows, lanes),
        name="stream_inner",
    )(velocity, flow, second)


def advance_stream_outer(flags, velocity, lower, upper, flow, second, rescale, result):
    _, planes, rows, lanes = velocity.shape
    return pl.pallas_call(
        stream_outer_kernel,
        out_shape=jax.ShapeDtypeStruct(velocity.shape, jnp.bfloat16),
        in_specs=[in_smem] + [in_hbm] * 3 + [in_vmem] * 3 + [in_hbm],
        out_specs=in_hbm,
        input_output_aliases={7: 0},
        scratch_shapes=[
            pltpu.VMEM((1, 2, 6, rows, lanes), jnp.bfloat16),
            pltpu.VMEM((4, rows, lanes), jnp.bfloat16),
            pltpu.VMEM((rows, 2 * lanes), jnp.float32),
            pltpu.SemaphoreType.DMA((4,)),
            pltpu.SemaphoreType.DMA((2,)),
        ],
        compiler_params=pltpu.CompilerParams(vmem_limit_bytes=EDGE_BYTES),
        cost_estimate=cost_of(1, 4, rows, lanes),
        name="stream_outer",
    )(flags, velocity, lower, upper, flow, second, rescale, result)


def pivot_kernel(diag, squared, out, pivots, sem):
    rows = diag.shape[0]
    chunks = squared.shape[0]

    def step(j, before):
        now = 1.0 / ((2.0 + diag[j]) + squared[...] - before)
        pivots[pl.ds(pl.multiple_of(j * chunks, chunks), chunks), :] = now
        return now

    lax.fori_loop(0, rows, step, jnp.zeros_like(squared[...]))
    copy = pltpu.make_async_copy(pivots, out.at[pl.ds(0, rows * chunks)], sem)
    copy.start()
    copy.wait()


def pivots_of(pressure_diag, squared):
    rows = pressure_diag.shape[0]
    chunks = squared.shape[0]
    return pl.pallas_call(
        pivot_kernel,
        out_shape=jax.ShapeDtypeStruct((PIVOT_SPACE * rows * chunks, LANES), jnp.float32),
        in_specs=[in_smem, in_vmem],
        out_specs=in_hbm,
        scratch_shapes=[pltpu.VMEM((rows * chunks, LANES), jnp.float32), pltpu.SemaphoreType.DMA],
        compiler_params=pltpu.CompilerParams(vmem_limit_bytes=ALL_BYTES),
        cost_estimate=pl.CostEstimate(flops=10**7, bytes_accessed=10**7, transcendentals=0),
        name="pivots",
    )(pressure_diag, squared)


def project_kernel(
    x, waves, first, pivots_in, there_in, back_in, result, out,
    there, back, pivots, folded, source, spectra, there_sems, back_sems, pivot_sem
):
    blocks, _, rows, _ = x.shape
    count = blocks * LANES
    half = count // 2
    chunks = count // LANES
    per = TILE // LANES
    groups = waves.shape[0]
    pairs = [(j // (groups // 2) * groups + j % (groups // 2), groups // 2) for j in range(groups)]
    pairs = [(a, a + step) for a, step in pairs]

    load_pivots = pltpu.make_async_copy(pivots_in.at[pl.ds(0, rows * chunks)], pivots, pivot_sem)
    loads = {t: pltpu.make_async_copy(there_in.at[t], there.at[t], there_sems.at[t]) for pair in pairs for t in pair}
    returns = [pltpu.make_async_copy(back_in.at[t], back.at[t], back_sems.at[t]) for t in range(back.shape[0])]
    for copy in loads.values():
        copy.start()
    load_pivots.start()
    for copy in returns:
        copy.start()

    def fold(g, carry):
        at = pl.ds(pl.multiple_of(g * LANES, LANES), LANES)
        for field in range(2):
            here = slice(field * rows, (field + 1) * rows)
            a = x[g, field].astype(jnp.float32)
            b = x[g + blocks // 2, field].astype(jnp.float32)
            folded[0, here, at] = (a + b).astype(jnp.bfloat16)
            folded[1, here, at] = (a - b).astype(jnp.bfloat16)
        return carry

    lax.fori_loop(0, blocks // 2, fold, 0)

    inverse_step = 1.0 / step_size
    for j, (a, b) in enumerate(pairs):
        loads[a].wait()
        loads[b].wait()
        lhs = folded.at[j // (groups // 2)]
        cosine = jnp.dot(lhs[...], there[a], preferred_element_type=jnp.float32)
        sine = jnp.dot(lhs[...], there[b], preferred_element_type=jnp.float32)
        wave = waves[j : j + 1, :]
        for tile, value in (
            (a, (cosine[:rows] + wave * sine[rows:]) * inverse_step),
            (b, (sine[:rows] - wave * cosine[rows:]) * inverse_step),
        ):
            for k in range(per):
                source[pl.ds(tile * per + k, rows, stride=chunks), :] = value[:, k * LANES : (k + 1) * LANES]

    load_pivots.wait()
    unroll = 8

    def forward(i, before):
        for k in range(unroll):
            at = pl.ds(pl.multiple_of((i * unroll + k) * chunks, chunks), chunks)
            before = pivots[at, :] * (source[at, :] + before)
            source[at, :] = before
        return before

    def backward(i, after):
        for k in range(unroll):
            j = rows - 1 - (i * unroll + k)
            at = pl.ds(pl.multiple_of(j * chunks, chunks), chunks)
            after = pivots[at, :] * after - source[at, :]
            source[at, :] = after
        return after

    zero = jnp.zeros((chunks, LANES), jnp.float32)
    lax.fori_loop(0, rows // unroll, forward, zero)
    lax.fori_loop(0, rows // unroll, backward, zero)

    twice = jnp.concatenate([first[...], first[...]], 1)
    for j, (a, b) in enumerate(pairs):
        wave = waves[j : j + 1, :]
        for tile, other, sign in ((a, b, -1.0), (b, a, 1.0)):
            pressure = jnp.concatenate(
                [source[pl.ds(tile * per + k, rows, stride=chunks), :] for k in range(per)], 1
            )
            high = pressure.astype(jnp.bfloat16)
            low = (pressure - high.astype(jnp.float32)).astype(jnp.bfloat16)
            both = jnp.concatenate([high, low], 0)
            spectra[:rows, tile * TILE : (tile + 1) * TILE] = jnp.dot(
                twice, both, preferred_element_type=jnp.float32
            ).astype(jnp.bfloat16)
            spectra[rows:, other * TILE : (other + 1) * TILE] = (sign * wave * pressure).astype(jnp.bfloat16)

    for tile in range(back.shape[0]):
        returns[tile].wait()
        even = jnp.dot(spectra[:, :half], back[tile, :half], preferred_element_type=jnp.float32)
        odd = jnp.dot(spectra[:, half:], back[tile, half:], preferred_element_type=jnp.float32)
        for k in range(per):
            at = slice(k * LANES, (k + 1) * LANES)
            g = tile * per + k
            for field in range(2):
                here = slice(field * rows, (field + 1) * rows)
                out[g, field] = (even[here, at] + odd[here, at]).astype(jnp.bfloat16)
                out[g + blocks // 2, field] = (even[here, at] - odd[here, at]).astype(jnp.bfloat16)


def project(x, pivots, wall_first, there, back, waves, result):
    blocks, _, rows, lanes = x.shape
    count = blocks * lanes
    return pl.pallas_call(
        project_kernel,
        out_shape=jax.ShapeDtypeStruct(x.shape, jnp.bfloat16),
        in_specs=[in_vmem] * 3 + [in_hbm] * 4,
        out_specs=in_vmem,
        scratch_shapes=[
            pltpu.VMEM(there.shape, jnp.bfloat16),
            pltpu.VMEM(back.shape, jnp.bfloat16),
            pltpu.VMEM((rows * count // LANES, LANES), jnp.float32),
            pltpu.VMEM((2, 2 * rows, count // 2), jnp.bfloat16),
            pltpu.VMEM((rows * count // LANES, LANES), jnp.float32),
            pltpu.VMEM((2 * rows, count), jnp.bfloat16),
            pltpu.SemaphoreType.DMA((there.shape[0],)),
            pltpu.SemaphoreType.DMA((back.shape[0],)),
            pltpu.SemaphoreType.DMA,
        ],
        compiler_params=pltpu.CompilerParams(vmem_limit_bytes=MOST_BYTES),
        cost_estimate=pl.CostEstimate(
            flops=4 * rows * count * count, bytes_accessed=4 * there.size + 8 * x.size, transcendentals=0
        ),
        name="project",
    )(x, waves, wall_first, pivots, there, back, result)


def correct_kernel(result_in, star, change_in, result, change, ready, loads, sems):
    planes = star.shape[1]
    group = 4
    pieces = [(field, pl.ds(start, group)) for start in range(0, planes, group) for field in range(2)]
    arrive = [
        pltpu.make_async_copy(change_in.at[pl.ds(start, group)], change.at[pl.ds(start, group)], loads.at[start // group])
        for start in range(0, planes, group)
    ]
    depart = [
        pltpu.make_async_copy(ready.at[field, here], result.at[field + 1, here], sems.at[i])
        for i, (field, here) in enumerate(pieces)
    ]
    for copy in arrive:
        copy.start()
    for i, (field, here) in enumerate(pieces):
        if field == 0:
            arrive[i // 2].wait()
        ready[field, here] = (
            star[field, here].astype(jnp.float32) + change[here, field].astype(jnp.float32)
        ).astype(jnp.bfloat16)
        depart[i].start()
    for copy in depart:
        copy.wait()


def correct(result, star, change):
    planes = star.shape[1]
    return pl.pallas_call(
        correct_kernel,
        out_shape=jax.ShapeDtypeStruct(result.shape, jnp.bfloat16),
        in_specs=[in_hbm, in_vmem, in_hbm],
        out_specs=in_hbm,
        input_output_aliases={0: 0},
        scratch_shapes=[
            pltpu.VMEM(change.shape, jnp.bfloat16),
            pltpu.VMEM(star.shape, jnp.bfloat16),
            pltpu.SemaphoreType.DMA((planes // 4,)),
            pltpu.SemaphoreType.DMA((2 * planes // 4,)),
        ],
        compiler_params=pltpu.CompilerParams(vmem_limit_bytes=LAST_BYTES),
        name="correct",
    )(result, star, change)


def across(x):
    blocks, fields, rows, lanes = x.shape
    moved = lax.all_to_all(x.reshape(blocks, fields * rows, lanes), "gz", split_axis=0, concat_axis=0, tiled=True)
    return moved.reshape(x.shape)


def on_device(velocity, base_flow, wall_second, wall_first, rescale, pressure_diag):
    groups, slabs = lax.axis_size("grp"), lax.axis_size("gx")
    place = lax.axis_index("grp") * slabs + lax.axis_index("gx")
    ends = groups * slabs - 1
    flags = jnp.stack(
        [
            jnp.where(place == 0, 1, jnp.where(place == slabs, 2, 0)),
            jnp.where((place == slabs - 1) | (place == ends), 1, 0),
        ]
    ).astype(jnp.int32)
    up = [(i, i + 1) for i in range(ends)]
    down = [(i + 1, i) for i in range(ends)]
    lower = lax.ppermute(velocity[1:, -2:], ("grp", "gx"), up)
    upper = lax.ppermute(velocity[1:, :2], ("grp", "gx"), down)
    stream_lower = lax.ppermute(velocity[:1, -2:], ("grp", "gx"), up)
    stream_upper = lax.ppermute(velocity[:1, :2], ("grp", "gx"), down)
    flow = jnp.broadcast_to(base_flow[:, None], (base_flow.shape[0], LANES))
    there, back, waves, squared = (jnp.asarray(t) for t in tables(lax.axis_size("gz") * velocity.shape[3]))

    star, send = advance_inner(velocity, flow, wall_second, wall_first)
    star, send = advance_outer(flags, velocity, lower, upper, flow, wall_second, wall_first, rescale, star, send)
    pencils = across(send)
    pivots = pivots_of(pressure_diag, squared)
    result = advance_stream_inner(velocity, flow, wall_second)
    result = advance_stream_outer(
        flags, velocity, stream_lower, stream_upper, flow, wall_second, rescale, result
    )
    change = across(project(pencils, pivots, wall_first, there, back, waves, result))
    return correct(result, star, change)


def solution(mesh):
    return jax.shard_map(
        on_device,
        mesh=mesh,
        in_specs=(P(None, ("grp", "gx"), None, "gz"), P(), P(), P(), P(), P()),
        out_specs=P(None, ("grp", "gx"), None, "gz"),
        check_vma=False,
    )
```
